256 devices in a mesh: pb: 8 (over y_lo, x), ia: 32 (over y_hi, z, core).
Axes of the slice: x: 4, y: 4 (y_hi: 2, y_lo: 2; y = y_hi * 2 + y_lo), z: 8, core: 2. Of those that a mesh axis runs over, the one named last changes fastest.
Arguments:
- query_feats: float32 [65536, 256], P(('pb', 'ia')), may hold values from -6 to 6
- item_table: float32 [16384, 256], P('pb'), may hold values from -6 to 6
- serve_ids: int32 [8, 32, 8, 512], P('pb', 'ia'), may hold values from 0 to 2047, as said below
- block_counts: int32 [8, 32, 8], P('pb', 'ia'), may hold values from 1 to 4, as said below
- item_refs: int32 [65536, 8], P(('pb', 'ia')), may hold values from 0 to 4095, as said below
- positive: int32 [65536], P(('pb', 'ia')), may hold values from 0 to 8191
- query_inner: float32 [256, 512], replicated, may hold values from -0.375 to 0.375
- query_outer: float32 [512, 256], replicated, may hold values from -0.25 to 0.25
- item_inner: float32 [256, 512], replicated, may hold values from -0.375 to 0.375
- item_outer: float32 [512, 256], replicated, may hold values from -0.25 to 0.25
Outputs:
- query_loss: float32 [65536], P(('pb', 'ia'))
- query_grad: float32 [65536, 256], P(('pb', 'ia'))
- table_grad: float32 [16384, 256], P(('pb', 'ia'))
The draws below stay inside these ranges and needn't reach their ends.
Inputs may be any that keep to these rules, and one draw needn't show every extreme that they name: serve_ids[o, j, p, c] is a row of pb shard o of the table, counted from the shard's first row; the 512 rows of one list are distinct. block_counts[p, j, o] is the number of leading 128-row blocks of list serve_ids[o, j, p] that are used; in every draw some list uses all 4 blocks. `item_refs`: an entry of an item on device (p, j) is o * 512 + c with c < 128 * block_counts[p, j, o].
All inputs are finite; a program needn't handle non-finite values.
Results may differ from the reference program's by a relative error of at most 0.00029.
Values sent between devices are 32-bit elements; how exact they have to be, the bound alone decides.
A program may use at most 128 MiB of HBM per device.

```python
import jax
import jax.numpy as jnp
from jax import lax

EMB = 256
FEAT = 256
HID = 512
Q_DEV = 256
TAB_DEV = 2048
REFS = 8
BLOCK = 128
NBLK = 4
CAP = 512
SLOTS = 4096
GROUP = 8192
QUERIES = 65536
ITEMS = 65536
TABLE = 16384
N_PB = 8
N_IA = 32


def draw_loads(key):
    level_key = jax.random.fold_in(key, 11)
    heavy_key = jax.random.fold_in(key, 12)
    pick_key = jax.random.fold_in(key, 13)
    spread_counts = jax.random.randint(level_key, (N_PB, N_IA, N_PB), 1, NBLK + 1)
    heavy_device = jax.random.randint(heavy_key, (N_PB, N_IA, 1), 0, 4) == 0
    counts = jnp.where(heavy_device, spread_counts, 1)
    chosen = jax.random.randint(pick_key, (3,), 0, jnp.array([N_PB, N_IA, N_PB], dtype=jnp.int32))
    counts = counts.at[chosen[0], chosen[1], chosen[2]].set(NBLK)
    return counts.astype(jnp.int32)


def draw_block_counts(key, part):
    loads = draw_loads(key)
    return loads


def draw_item_refs(key, part):
    loads = draw_loads(key)
    key = jax.random.fold_in(key, 5)
    owner_key = jax.random.fold_in(key, 21)
    row_key = jax.random.fold_in(key, 22)
    device_of = jnp.arange(ITEMS, dtype=jnp.int32) // Q_DEV
    owner_pick = jax.random.randint(owner_key, (ITEMS, REFS), 0, N_PB)
    row_draw = jax.random.randint(row_key, (ITEMS, REFS), 0, 1048576)
    row_limit = loads[(device_of // N_IA)[:, None], (device_of % N_IA)[:, None], owner_pick] * BLOCK
    return (owner_pick * CAP + row_draw % row_limit).astype(jnp.int32)


def draw_serve_ids(key, part):
    key = jax.random.fold_in(key, 7)
    list_keys = jax.random.split(key, N_PB * N_IA * N_PB)
    picked = jax.vmap(lambda one_key: jax.random.permutation(one_key, TAB_DEV)[:CAP])(list_keys)
    return picked.reshape(N_PB, N_IA, N_PB, CAP).astype(jnp.int32)


def place_ends(result, key, low, largest):
    place = [jax.random.randint(jax.random.fold_in(key, axis), (), 0, length) for axis, length in enumerate(result.shape)]
    widest = result.shape.index(max(result.shape))
    beside = place[:widest] + [(place[widest] + 1) % result.shape[widest]] + place[widest + 1:]
    return result.at[tuple(place)].set(low).at[tuple(beside)].set(largest)


def block_scale(own_key, extent, cuts, low, largest):
    level = 1.0
    for dim, shards_of in cuts:
        draws = jax.random.uniform(jax.random.fold_in(jax.random.fold_in(own_key, 6), dim), (shards_of,), jnp.float32, low / len(cuts), largest / len(cuts))
        level = level * jnp.repeat(jnp.exp(draws), extent[dim] // shards_of).reshape((-1,) + (1,) * (len(extent) - 1 - dim))
    return level


def bell_draw(own_key, extent, spread, reach, pieces=(), kind=jnp.bfloat16):
    values = jax.random.normal(own_key, extent, jnp.float32) * spread
    if len(pieces) > 0:
        values = block_scale(own_key, extent, pieces, -0.22, 0.18) * values
    return jnp.clip(values, min=-reach, max=reach).astype(kind)


def setup_inputs(seed: int = 0) -> dict:
    splits = jax.random.split(jax.random.key(seed), 11)
    query_feats = bell_draw(splits[0], (QUERIES, FEAT), 1.0, 6.0, ((0, 256),), jnp.float32)
    item_table = bell_draw(splits[1], (TABLE, FEAT), 1.0, 6.0, ((0, 8),), jnp.float32)
    serve_ids = draw_serve_ids(jax.random.fold_in(splits[10], 71), 0)
    block_counts = draw_block_counts(jax.random.fold_in(splits[10], 71), 0)
    item_refs = draw_item_refs(jax.random.fold_in(splits[10], 71), 0)
    positive = place_ends(jax.random.randint(splits[5], (QUERIES,), 0, GROUP), jax.random.fold_in(splits[5], 1), 0, GROUP - 1).astype(jnp.int32)
    query_inner = bell_draw(splits[6], (FEAT, HID), FEAT ** -0.5, 0.375, (), jnp.float32)
    query_outer = bell_draw(splits[7], (HID, EMB), HID ** -0.5, 0.25, (), jnp.float32)
    item_inner = bell_draw(splits[8], (FEAT, HID), FEAT ** -0.5, 0.375, (), jnp.float32)
    item_outer = bell_draw(splits[9], (HID, EMB), HID ** -0.5, 0.25, (), jnp.float32)
    return {"query_feats": query_feats, "item_table": item_table, "serve_ids": serve_ids, "block_counts": block_counts, "item_refs": item_refs, "positive": positive, "query_inner": query_inner, "query_outer": query_outer, "item_inner": item_inner, "item_outer": item_outer}


inverse_temp = 20.0
epsilon = 1e-06
highest = lax.Precision.HIGHEST

def matmul(left, right):
    return jnp.dot(left, right, preferred_element_type=jnp.float32, precision=highest)

def matmul_nt(left, right):
    return lax.dot_general(left, right, (((1,), (1,)), ((), ())), precision=highest, preferred_element_type=jnp.float32)

def matmul_tn(left, right):
    return lax.dot_general(left, right, (((0,), (0,)), ((), ())), precision=highest, preferred_element_type=jnp.float32)

def normalize(raw_rows):
    return raw_rows * lax.rsqrt(lax.optimization_barrier(jnp.sum(raw_rows * raw_rows, axis=1, keepdims=True)) + epsilon)

def query_tower(features, query_inner, query_outer):
    return normalize(matmul(jax.nn.gelu(matmul(features, query_inner), approximate=False), query_outer))

def item_head(pooled, item_outer):
    return normalize(matmul(pooled, item_outer))

def reference(query_feats, item_table, serve_ids, block_counts, item_refs, positive, query_inner, query_outer, item_inner, item_outer):
    devices = N_PB * N_IA
    row_lists = jnp.transpose(serve_ids, (2, 1, 0, 3)) + (jnp.arange(N_PB, dtype=jnp.int32) * TAB_DEV)[None, None, :, None]
    row_lists = row_lists.reshape(devices, SLOTS).astype(jnp.int32)
    valid_rows = (jnp.arange(CAP, dtype=jnp.int32)[None, None, None, :] < BLOCK * block_counts[..., None]).reshape(devices, SLOTS)
    refs_dev = item_refs.reshape(devices, Q_DEV, REFS)

    def slot_features(row_ids, live_rows):
        return jnp.where(live_rows[:, None], item_table[row_ids], 0.0)

    def item_embed(features, refs_here):
        hidden = jax.nn.gelu(matmul(features, item_inner), approximate=False)
        return item_head(lax.optimization_barrier(jnp.sum(hidden[refs_here], axis=1)), item_outer)

    def embed_device(packed):
        return item_embed(slot_features(packed[0], packed[1]), packed[2])
    item_emb = lax.map(embed_device, (row_lists, valid_rows, refs_dev)).reshape(ITEMS, EMB)
    query_emb, query_back = jax.vjp(lambda inputs: query_tower(inputs, query_inner, query_outer), query_feats)

    def group_terms(packed):
        queries, group_items, group_positive = packed
        logits = inverse_temp * matmul_nt(queries, group_items)
        log_total = jnp.log(lax.optimization_barrier(jnp.sum(jnp.exp(logits), axis=1)))
        positive_emb = group_items[group_positive]
        losses = log_total - inverse_temp * lax.optimization_barrier(jnp.sum(queries * positive_emb, axis=1))
        probability = jnp.exp(logits - log_total[:, None])
        coefficient = probability.at[jnp.arange(GROUP), group_positive].add(-1.0)
        grad_queries = inverse_temp * matmul(coefficient, group_items)
        grad_items = inverse_temp * matmul_tn(coefficient, queries)
        return (losses, grad_queries, grad_items)
    losses, grad_queries, grad_items = lax.map(group_terms, (query_emb.reshape(N_PB, GROUP, EMB), item_emb.reshape(N_PB, GROUP, EMB), positive.reshape(N_PB, GROUP)))
    query_loss = losses.reshape(QUERIES)
    query_grad = query_back(grad_queries.reshape(QUERIES, EMB))[0]

    def add_device(totals, packed):
        row_ids, live_rows, refs_here, grad_emb = packed
        features = slot_features(row_ids, live_rows)
        back_fn = jax.vjp(lambda inputs: item_embed(inputs, refs_here), features)[1]
        grad_features = back_fn(grad_emb)[0]
        return (totals.at[row_ids].add(jnp.where(live_rows[:, None], grad_features, 0.0)), jnp.zeros((), jnp.float32))
    table_grad = lax.scan(add_device, jnp.zeros((TABLE, FEAT), jnp.float32), (row_lists, valid_rows, refs_dev, grad_items.reshape(devices, Q_DEV, EMB)))[0]
    return (query_loss, query_grad, table_grad)
```

```python
import functools

import jax
import jax.numpy as jnp
from jax import lax
from jax.experimental import pallas as pl
from jax.experimental.pallas import tpu as pltpu
from jax.sharding import PartitionSpec as P

BLOCK = 128
CAP = 512
MESH = pl.DeviceIdType.MESH
VM = pltpu.VMEM
DMA = pltpu.SemaphoreType.DMA
f32 = jnp.float32
bf16 = jnp.bfloat16

inverse_temp = 20.0
epsilon = 1e-06

NN = (((1,), (0,)), ((), ()))
NT = (((1,), (1,)), ((), ()))


def split(v):
    hi = v.astype(bf16)
    return hi, (v - hi.astype(f32)).astype(bf16)


def dot(a, b, dims=NN):
    return lax.dot_general(a, b, dims, preferred_element_type=f32)


def dot3(a, b, dims=NN):
    return dot(a[0], b[0], dims) + (dot(a[0], b[1], dims) + dot(a[1], b[0], dims))


def normal_cdf(v):
    return 0.5 * (1.0 + lax.erf(v * 0.7071067811865476))


def gelu(v):
    return v * normal_cdf(v)


def gelu_slope(v):
    return normal_cdf(v) + v * (0.3989422804014327 * jnp.exp(-0.5 * v * v))


def place():
    p, j = lax.axis_index("pb"), lax.axis_index("ia")
    return p, j, p % 4, p // 4, j // 16, (j // 2) % 8, j % 2


def greet(peers):
    barrier = pltpu.get_barrier_semaphore()
    for peer in peers:
        pl.semaphore_signal(barrier, inc=1, device_id=peer, device_id_type=MESH)
    pl.semaphore_wait(barrier, len(peers))


def push(src, dst, send, recv, peer):
    return pltpu.make_async_remote_copy(
        src_ref=src, dst_ref=dst, send_sem=send, recv_sem=recv, device_id=peer, device_id_type=MESH
    )


def pool_kernel(
    refs_ref,
    lists_ref,
    pos_ref,
    table_ref,
    inner_ref,
    outer_ref,
    qf_ref,
    qi_ref,
    qo_ref,
    raw_ref,
    qpre_ref,
    qraw_ref,
    ct_ref,
    qall_ref,
    posall_ref,
    refs_all,
    zh,
    zl,
    innh,
    innl,
    outh,
    outl,
    qemb,
    ct,
    part,
    got,
    refs_sem,
    pos_sem,
    q_sem,
    part_sem,
    ct_sem,
    own_sem,
):
    p, j, x, yl, yh, z, core = place()

    def zdev(d):
        return (p, (yh * 8 + (z + d) % 8) * 2 + core)

    def pbdev(dy, dx):
        return (((yl + dy) % 2) * 4 + (x + dx) % 4, j)

    pb_peers = [(dy, dx) for dy in range(2) for dx in range(4) if dy or dx]
    greet([pbdev(*d) for d in pb_peers] + [zdev(d) for d in range(1, 8)])

    refs_cp = [
        push(refs_ref, refs_all.at[p], refs_sem.at[0, i], refs_sem.at[1, i], pbdev(*d))
        for i, d in enumerate(pb_peers)
    ]
    pos_cp = [
        push(pos_ref, posall_ref.at[z], pos_sem.at[0, i], pos_sem.at[1, i], zdev(i + 1))
        for i in range(7)
    ]
    for c in refs_cp + pos_cp:
        c.start()
    refs_all[p] = refs_ref[...]
    own_pos = pltpu.make_async_copy(pos_ref, posall_ref.at[z], own_sem.at[0])
    own_pos.start()

    qpre = dot3(split(qf_ref[...]), split(qi_ref[...]))
    qpre_ref[...] = qpre
    qraw = dot3(split(gelu(qpre)), split(qo_ref[...]))
    qraw_ref[...] = qraw
    qemb[...] = qraw * lax.rsqrt(jnp.sum(qraw * qraw, axis=1, keepdims=True) + epsilon)
    own_q = pltpu.make_async_copy(qemb, qall_ref.at[z], own_sem.at[1])
    own_q.start()

    def right(s):
        b = (z + 8 - s) % 8
        src = qemb if s == 0 else qall_ref.at[b]
        return push(src, qall_ref.at[b], q_sem.at[0, s], q_sem.at[1, s], zdev(1))

    def left(s):
        b = (z + s) % 8
        src = qemb if s == 0 else qall_ref.at[b]
        return push(src, qall_ref.at[b], q_sem.at[0, 4 + s], q_sem.at[1, 4 + s], zdev(7))

    right(0).start()
    left(0).start()

    ih, il = split(jnp.transpose(inner_ref[...]))
    innh[...], innl[...] = ih, il
    oh, ol = split(jnp.transpose(outer_ref[...]))
    outh[...], outl[...] = oh, ol

    def rows(t, carry):
        r = pl.ds(pl.multiple_of(t * 256, 256), 256)
        hid = dot3((innh[...], innl[...]), split(table_ref[r, :]), NT)
        h, l = split(dot3((outh[...], outl[...]), split(gelu(hid))))
        zh[:, r] = h
        zl[:, r] = l
        return carry

    lax.fori_loop(0, 8, rows, 0)

    for c in refs_cp:
        c.wait()

    def piece(s):
        k = s // 2
        dx = (1 - k // 2) * (2 + k) + (k // 2) * (3 - k)
        dy = 1 - s % 2
        return pbdev(dy, dx)

    def part_cp(s):
        dest = piece(s)
        return push(part.at[s], got.at[p], part_sem.at[0, s], part_sem.at[1, s], dest)

    def ct_cp(s):
        b = piece(s)[0]
        return pltpu.make_async_copy(ct.at[b], ct_ref.at[b], ct_sem.at[s])

    def pieces(s, carry):
        b = piece(s)[0]
        refs = refs_all[b]
        slot = lax.broadcasted_iota(jnp.int32, (CAP, 256), 0) + p * CAP
        uses = jnp.zeros((CAP, 256), f32)
        for k in range(8):
            uses = uses + jnp.where(slot == refs[k : k + 1, :], 1.0, 0.0)
        uses = uses.astype(bf16)
        listed = lists_ref[pl.ds(b, 1), :]
        total = jnp.zeros((256, 256), f32)
        for t in range(8):
            row = lax.broadcasted_iota(jnp.int32, (256, CAP), 0) + t * 256
            pick = jnp.where(row == listed, 1.0, 0.0).astype(bf16)
            times = dot(pick, uses).astype(bf16)
            ct[b, t * 256 : (t + 1) * 256, :] = times
            w = slice(t * 256, (t + 1) * 256)
            total = total + (dot(zh[:, w], times) + dot(zl[:, w], times))
        ct_cp(s).start()

        @pl.when(s < 7)
        def _():
            part[s] = total
            part_cp(s).start()

        @pl.when(s == 7)
        def _():
            got[p] = total

        return carry

    lax.fori_loop(0, 3, pieces, 0)
    right(0).wait_recv()
    right(1).start()
    left(0).wait_recv()
    left(1).start()
    lax.fori_loop(3, 6, pieces, 0)
    right(1).wait_recv()
    right(2).start()
    left(1).wait_recv()
    left(2).start()
    lax.fori_loop(6, 8, pieces, 0)
    right(2).wait_recv()
    right(3).start()
    left(2).wait_recv()
    for s in range(7):
        part_cp(s).wait()
    acc = got[0]
    for b in range(1, 8):
        acc = acc + got[b]
    raw_ref[...] = jnp.transpose(acc)
    right(3).wait_recv()
    for s in range(4):
        right(s).wait_send()
    for s in range(3):
        left(s).wait_send()
    for c in pos_cp:
        c.wait()
    own_pos.wait()
    own_q.wait()
    for s in range(8):
        ct_cp(s).wait()


def loss_kernel(
    raw_ref,
    q_ref,
    pos_ref,
    loss_ref,
    draw_ref,
    dq_ref,
    items,
    qh,
    ql,
    iTh,
    iTl,
    ex,
    stats,
    stats_all,
    ditem,
    dsend,
    dgot,
    item_sem,
    stat_sem,
    d_sem,
):
    p, j, x, yl, yh, z, core = place()

    def at(dyh, dz, dc):
        return (p, (((yh + dyh) % 2) * 8 + (z + dz) % 8) * 2 + (core + dc) % 2)

    near = [(0, 1), (1, 0), (1, 1)]
    greet([at(a, 0, c) for a, c in near] + [at(0, d, 0) for d in range(1, 8)])

    raw = raw_ref[...]
    inv_norm = lax.rsqrt(jnp.sum(raw * raw, axis=1, keepdims=True) + epsilon)
    emb = raw * inv_norm
    items[0] = emb
    item_cp = [
        push(items.at[0], items.at[i + 1], item_sem.at[0, i], item_sem.at[1, i], at(a, 0, c))
        for i, (a, c) in enumerate(near)
    ]
    for i in (1, 2, 0):
        item_cp[i].start()
    for b in range(8):
        h, l = split(q_ref[b])
        qh[b], ql[b] = h, l
    stats[...] = jnp.zeros((16, 256), f32)

    def base(i):
        a, c = ([(0, 0)] + near)[i]
        return (((yh + a) % 2) * 8 + z) * 2 + (core + c) % 2

    def logits(i):
        here = items[i]
        ih, il = split(here)
        th, tl = split(jnp.transpose(here))
        iTh[i], iTl[i] = th, tl
        number = lax.broadcasted_iota(jnp.int32, (256, 256), 0) + base(i) * 256

        def step(b, carry):
            lg = inverse_temp * dot3((ih, il), (qh[b], ql[b]), NT)
            e = jnp.exp(lg)
            ex[i, b] = e
            r = pl.ds(b, 1)
            stats[r, :] = stats[r, :] + jnp.sum(e, axis=0, keepdims=True)
            hit = pos_ref[b][0:1, :] == number
            r8 = pl.ds(b + 8, 1)
            stats[r8, :] = stats[r8, :] + jnp.sum(jnp.where(hit, lg, 0.0), axis=0, keepdims=True)
            return carry

        lax.fori_loop(0, 8, step, 0)

    logits(0)
    for i in range(3):
        item_cp[i].wait_recv()
        logits(i + 1)

    stat_cp = [
        push(stats, stats_all.at[z], stat_sem.at[0, i], stat_sem.at[1, i], at(0, i + 1, 0))
        for i in range(7)
    ]
    for c in stat_cp:
        c.start()
    stats_all[z] = stats[...]
    for c in stat_cp:
        c.wait()
    both = stats_all[0]
    for b in range(1, 8):
        both = both + stats_all[b]
    stats[...] = both
    loss_ref[...] = jnp.log(stats[pl.ds(z, 1), :]) - stats[pl.ds(z + 8, 1), :]
    stats[0:8, :] = inverse_temp / both[0:8, :]

    def grads(i, first):
        number = lax.broadcasted_iota(jnp.int32, (256, 256), 0) + base(i) * 256
        th, tl = iTh[i], iTl[i]

        def step(b, total):
            hit = pos_ref[b][0:1, :] == number
            coef = ex[i, b] * stats[pl.ds(b, 1), :] - jnp.where(hit, inverse_temp, 0.0)
            c = split(coef)
            back = dot3((th, tl), c)
            if first:
                dq_ref[b] = back
            else:
                dq_ref[b] = dq_ref[b] + back
            return total + dot3(c, (qh[b], ql[b]))

        return lax.fori_loop(0, 8, step, jnp.zeros((256, 256), f32))

    to_sib = [
        push(dsend.at[i], dgot.at[i], d_sem.at[0, i], d_sem.at[1, i], at(0, 0, 1)) for i in range(2)
    ]
    across = push(dsend.at[2], dgot.at[2], d_sem.at[0, 2], d_sem.at[1, 2], at(1, 0, 0))
    dsend[0] = grads(3, True)
    to_sib[0].start()
    mine = grads(2, False)
    to_sib[0].wait_recv()
    dsend[2] = mine + dgot[0]
    across.start()
    dsend[1] = grads(1, False)
    to_sib[1].start()
    mine = grads(0, False)
    to_sib[1].wait_recv()
    mine = mine + dgot[1]
    across.wait_recv()
    d = mine + dgot[2]
    draw_ref[...] = inv_norm * (d - emb * jnp.sum(emb * d, axis=1, keepdims=True))
    for c in item_cp:
        c.wait_send()
    for c in to_sib:
        c.wait_send()
    across.wait_send()


def table_kernel(
    draw_ref,
    dq_ref,
    qpre_ref,
    qraw_ref,
    table_ref,
    inner_ref,
    outer_ref,
    qi_ref,
    qo_ref,
    ct_ref,
    qg_ref,
    tg_ref,
    d_all,
    ct,
    acc,
    csend,
    cgot,
    zsend,
    zgot,
    ysend,
    ygot,
    qsend,
    qgot,
    ct_sem,
    d_sem,
    c_sem,
    z_sem,
    y_sem,
    q_sem,
):
    p, j, x, yl, yh, z, core = place()

    def at(dyh, dz, dc):
        return (p, (((yh + dyh) % 2) * 8 + (z + dz) % 8) * 2 + (core + dc) % 2)

    def pbdev(dy, dx):
        return (((yl + dy) % 2) * 4 + (x + dx) % 4, j)

    order = [(1, 0), (0, 1), (0, 3), (0, 2), (1, 1), (1, 3), (1, 2)]
    greet([pbdev(*d) for d in order] + [at(0, 1, 0), at(0, 7, 0), at(0, 0, 1), at(1, 0, 0)])

    load = [pltpu.make_async_copy(ct_ref.at[b], ct.at[b], ct_sem.at[b]) for b in range(8)]
    for c in load:
        c.start()
    d_cp = [
        push(draw_ref, d_all.at[p], d_sem.at[0, i], d_sem.at[1, i], pbdev(*d))
        for i, d in enumerate(order)
    ]
    for c in d_cp:
        c.start()
    d_all[p] = draw_ref[...]

    def q_right(s):
        return push(qsend.at[s], qgot.at[s], q_sem.at[0, s], q_sem.at[1, s], at(0, 1, 0))

    def q_left(s):
        return push(qsend.at[4 + s], qgot.at[4 + s], q_sem.at[0, 4 + s], q_sem.at[1, 4 + s], at(0, 7, 0))

    def q_step(s):
        mine = dq_ref[(z + 4 - s) % 8]
        if s:
            q_right(s - 1).wait_recv()
            mine = mine + qgot[s - 1]
        qsend[s] = mine
        q_right(s).start()
        if s < 3:
            mine = dq_ref[(z + 5 + s) % 8]
            if s:
                q_left(s - 1).wait_recv()
                mine = mine + qgot[4 + s - 1]
            qsend[4 + s] = mine
            q_left(s).start()

    q_step(0)
    for c in load:
        c.wait()

    def add_rows(b, first):
        dh, dl = split(d_all[b])

        def step(t, carry):
            r = pl.ds(pl.multiple_of(t * 256, 256), 256)
            c = ct[b, r, :]
            new = (dot(c, dh) + dot(c, dl)).reshape(2, 2, 64, 256)
            here = pl.ds(t * 2, 2)
            if first:
                acc[here] = new
            else:
                acc[here] = acc[here] + new
            return carry

        lax.fori_loop(0, 8, step, 0)

    add_rows(p, True)
    for i in range(7):
        d_cp[i].wait_recv()
        dy, dx = order[i]
        add_rows(((yl + dy) % 2) * 4 + (x + 4 - dx) % 4, False)
        if i == 2:
            q_step(1)
        if i == 4:
            q_step(2)

    q_step(3)
    c_cp = push(csend, cgot, c_sem.at[0], c_sem.at[1], at(0, 0, 1))
    csend[...] = acc[:, 1 - core]
    c_cp.start()
    c_cp.wait_recv()

    def mine_at(d, a):
        q = a * 8 + (z + d) % 8
        return acc[q, core] + cgot[q]

    def z_right(s, a):
        k = 2 * s + a
        return push(zsend.at[k], zgot.at[k], z_sem.at[0, k], z_sem.at[1, k], at(0, 1, 0))

    def z_left(s, a):
        k = 8 + 2 * s + a
        return push(zsend.at[k], zgot.at[k], z_sem.at[0, k], z_sem.at[1, k], at(0, 7, 0))

    for s in range(4):
        for a in range(2):
            v = mine_at(4 - s, a)
            if s:
                z_right(s - 1, a).wait_recv()
                v = v + zgot[2 * (s - 1) + a]
            zsend[2 * s + a] = v
            z_right(s, a).start()
            if s < 3:
                v = mine_at(5 + s, a)
                if s:
                    z_left(s - 1, a).wait_recv()
                    v = v + zgot[8 + 2 * (s - 1) + a]
                zsend[8 + 2 * s + a] = v
                z_left(s, a).start()

    q_right(3).wait_recv()
    q_left(2).wait_recv()
    d = jnp.transpose(dq_ref[z] + (qgot[3] + qgot[6]))
    qraw = qraw_ref[...]
    inv_norm = lax.rsqrt(jnp.sum(qraw * qraw, axis=1, keepdims=True) + epsilon)
    emb = qraw * inv_norm
    d = inv_norm * (d - emb * jnp.sum(emb * d, axis=1, keepdims=True))
    d = dot3(split(d), split(qo_ref[...]), NT) * gelu_slope(qpre_ref[...])
    qg_ref[...] = dot3(split(d), split(qi_ref[...]), NT)

    inner = split(inner_ref[...])
    own = table_ref[pl.ds(pl.multiple_of(j * 64, 64), 64), :]
    slope = gelu_slope(dot3(split(own), inner))

    for a in range(2):
        z_left(2, a).wait_recv()
        z_right(3, a).wait_recv()
    y_cp = push(ysend, ygot, y_sem.at[0], y_sem.at[1], at(1, 0, 0))

    def block(a):
        return acc[a * 8 + z, core] + cgot[a * 8 + z] + (zgot[6 + a] + zgot[12 + a])

    ysend[...] = block(1 - yh)
    y_cp.start()
    v = block(yh)
    y_cp.wait()
    v = v + ygot[...]
    d = dot3(split(v), split(outer_ref[...]), NT) * slope
    tg_ref[...] = dot3(split(d), inner, NT)

    for c in d_cp:
        c.wait_send()
    c_cp.wait_send()
    for s in range(4):
        q_right(s).wait_send()
        for a in range(2):
            z_right(s, a).wait_send()
    for s in range(3):
        q_left(s).wait_send()
        for a in range(2):
            z_left(s, a).wait_send()


def per_device(
    query_feats,
    item_table,
    serve_ids,
    block_counts,
    item_refs,
    positive,
    query_inner,
    query_outer,
    item_inner,
    item_outer,
):
    lists = serve_ids[0, 0]
    limits = BLOCK * block_counts[0, 0]
    owner = item_refs // CAP
    limit = jnp.zeros_like(item_refs)
    for o in range(8):
        limit = jnp.where(owner == o, limits[o], limit)
    refs = jnp.where(item_refs - owner * CAP < limit, item_refs, -1).T
    pos = jnp.broadcast_to(positive[None, :], (8, 256))

    vm = pl.BlockSpec(memory_space=pltpu.VMEM)
    hbm = pl.BlockSpec(memory_space=pl.ANY)

    def shape(*dims, dtype=f32):
        return jax.ShapeDtypeStruct(dims, dtype)

    def params(number):
        return pltpu.CompilerParams(
            collective_id=number, has_side_effects=True, vmem_limit_bytes=56 << 20
        )

    raw, qpre, qraw, ct, qall, posall = pl.pallas_call(
        pool_kernel,
        name="pool",
        out_shape=[
            shape(256, 256),
            shape(256, 512),
            shape(256, 256),
            shape(8, 2048, 256, dtype=bf16),
            shape(8, 256, 256),
            shape(8, 8, 256, dtype=jnp.int32),
        ],
        in_specs=[vm] * 9,
        out_specs=[vm, vm, vm, hbm, hbm, hbm],
        scratch_shapes=[
            VM((8, 8, 256), jnp.int32),
            VM((256, 2048), bf16),
            VM((256, 2048), bf16),
            VM((512, 256), bf16),
            VM((512, 256), bf16),
            VM((256, 512), bf16),
            VM((256, 512), bf16),
            VM((256, 256), f32),
            VM((8, 2048, 256), bf16),
            VM((7, 256, 256), f32),
            VM((8, 256, 256), f32),
            DMA((2, 7)),
            DMA((2, 7)),
            DMA((2, 7)),
            DMA((2, 7)),
            DMA((8,)),
            DMA((2,)),
        ],
        compiler_params=params(1),
    )(
        refs,
        lists,
        pos,
        item_table,
        item_inner,
        item_outer,
        query_feats,
        query_inner,
        query_outer,
    )

    loss, draw, dq = pl.pallas_call(
        loss_kernel,
        name="loss",
        out_shape=[shape(1, 256), shape(256, 256), shape(8, 256, 256)],
        in_specs=[vm] * 3,
        out_specs=[vm] * 3,
        scratch_shapes=[
            VM((4, 256, 256), f32),
            VM((8, 256, 256), bf16),
            VM((8, 256, 256), bf16),
            VM((4, 256, 256), bf16),
            VM((4, 256, 256), bf16),
            VM((4, 8, 256, 256), f32),
            VM((16, 256), f32),
            VM((8, 16, 256), f32),
            VM((256, 256), f32),
            VM((3, 256, 256), f32),
            VM((3, 256, 256), f32),
            DMA((2, 3)),
            DMA((2, 7)),
            DMA((2, 3)),
        ],
        compiler_params=params(2),
    )(raw, qall, posall)

    query_grad, table_grad = pl.pallas_call(
        table_kernel,
        name="table",
        out_shape=[shape(256, 256), shape(64, 256)],
        in_specs=[vm] * 9 + [hbm],
        out_specs=[vm] * 2,
        scratch_shapes=[
            VM((8, 256, 256), f32),
            VM((8, 2048, 256), bf16),
            VM((16, 2, 64, 256), f32),
            VM((16, 64, 256), f32),
            VM((16, 64, 256), f32),
            VM((14, 64, 256), f32),
            VM((14, 64, 256), f32),
            VM((64, 256), f32),
            VM((64, 256), f32),
            VM((7, 256, 256), f32),
            VM((7, 256, 256), f32),
            DMA((8,)),
            DMA((2, 7)),
            DMA((2,)),
            DMA((2, 14)),
            DMA((2,)),
            DMA((2, 7)),
        ],
        compiler_params=params(3),
    )(draw, dq, qpre, qraw, item_table, item_inner, item_outer, query_inner, query_outer, ct)
    return (loss.reshape(256), query_grad, table_grad)


def solution(mesh):
    placed = (
        P(("pb", "ia"), None),
        P("pb", None),
        P("pb", "ia", None, None),
        P("pb", "ia", None),
        P(("pb", "ia"), None),
        P(("pb", "ia")),
        P(),
        P(),
        P(),
        P(),
    )
    return jax.shard_map(
        per_device,
        mesh=mesh,
        in_specs=placed,
        out_specs=(P(("pb", "ia")), P(("pb", "ia"), None), P(("pb", "ia"), None)),
        check_vma=False,
    )
```

```python
import jax
import jax.numpy as jnp
from jax import lax
from jax.experimental import pallas as pl
from jax.experimental.pallas import tpu as pltpu
from jax.sharding import PartitionSpec as P

BLOCK = 128
CAP = 512
MESH = pl.DeviceIdType.MESH
VM = pltpu.VMEM
DMA = pltpu.SemaphoreType.DMA
f32 = jnp.float32
bf16 = jnp.bfloat16

inverse_temp = 20.0
epsilon = 1e-06

NN = (((1,), (0,)), ((), ()))
NT = (((1,), (1,)), ((), ()))


def split(v):
    hi = v.astype(bf16)
    return hi, (v - hi.astype(f32)).astype(bf16)


def dot(a, b, dims=NN):
    return lax.dot_general(a, b, dims, preferred_element_type=f32)


def lhs(v):
    h, l = split(v)
    return jnp.concatenate([h, h, l], axis=1)


def rhs(v, axis):
    h, l = split(v)
    return jnp.concatenate([h, l, h], axis=axis)


def dot3(a, b, dims=NN):
    return dot(lhs(a), rhs(b, dims[0][1][0]), dims)


def normal_cdf(v):
    return 0.5 * (1.0 + lax.erf(v * 0.7071067811865476))


def gelu(v):
    return v * normal_cdf(v)


def gelu_slope(v):
    return normal_cdf(v) + v * (0.3989422804014327 * jnp.exp(-0.5 * v * v))


def place():
    p, j = lax.axis_index("pb"), lax.axis_index("ia")
    return p, j, p % 4, p // 4, j // 16, (j // 2) % 8, j % 2


def greet(peers):
    barrier = pltpu.get_barrier_semaphore()
    for peer in peers:
        pl.semaphore_signal(barrier, inc=1, device_id=peer, device_id_type=MESH)
    pl.semaphore_wait(barrier, len(peers))


def push(src, dst, sems, k, peer):
    return pltpu.make_async_remote_copy(
        src_ref=src,
        dst_ref=dst,
        send_sem=sems.at[0, k],
        recv_sem=sems.at[1, k],
        device_id=peer,
        device_id_type=MESH,
    )


def step_kernel(
    refs_ref,
    counts_ref,
    lists_ref,
    pos_ref,
    table_ref,
    inner_ref,
    outer_ref,
    qf_ref,
    qi_ref,
    qo_ref,
    loss_ref,
    qg_ref,
    tg_ref,
    live,
    refs_all,
    posb,
    pos_all,
    zcat,
    inncat,
    outcat,
    qall,
    qpre_s,
    qraw_s,
    ct,
    part,
    got,
    items,
    qn,
    qr,
    tcat,
    ex,
    stats,
    stats_all,
    dsend,
    dgot,
    draw,
    d_all,
    dq,
    acc,
    cgot,
    zsend,
    zgot,
    ysend,
    ygot,
    qsend,
    qgot,
    refs_sem,
    pos_sem,
    ring_sem,
    part_sem,
    item_sem,
    stat_sem,
    near_sem,
    d_sem,
    c_sem,
    z_sem,
    y_sem,
    q_sem,
):
    p, j, x, yl, yh, z, core = place()

    def at(dyh, dz, dc):
        return (p, (((yh + dyh) % 2) * 8 + (z + dz) % 8) * 2 + (core + dc) % 2)

    def pbdev(dy, dx):
        return (((yl + dy) % 2) * 4 + (x + dx) % 4, j)

    order = [(1, 0), (0, 1), (0, 3), (0, 2), (1, 1), (1, 3), (1, 2)]
    pb_from = [((yl + dy) % 2) * 4 + (x + 4 - dx) % 4 for dy, dx in order]
    near = [(0, 1), (1, 0), (1, 1)]
    greet(
        [pbdev(*d) for d in order]
        + [at(0, d, 0) for d in range(1, 8)]
        + [at(0, 0, 1), at(1, 0, 0)]
    )

    refs = refs_ref[...]
    owner = refs // CAP
    limit = jnp.zeros((8, 256), jnp.int32)
    for o in range(8):
        limit = jnp.where(owner == o, BLOCK * counts_ref[o], limit)
    live[...] = jnp.where(refs - owner * CAP < limit, refs, -1)
    refs_all[p] = live[...]
    posb[...] = jnp.broadcast_to(pos_ref[...], (8, 256))
    pos_all[z] = posb[...]
    refs_cp = [push(live, refs_all.at[p], refs_sem, i, pbdev(*d)) for i, d in enumerate(order)]
    pos_cp = [push(posb, pos_all.at[z], pos_sem, i, at(0, i + 1, 0)) for i in range(7)]
    for c in refs_cp + pos_cp:
        c.start()

    qpre = dot3(qf_ref[...], qi_ref[...])
    qpre_s[...] = qpre
    qraw = dot3(gelu(qpre), qo_ref[...])
    qraw_s[...] = qraw
    qall[z] = qraw * lax.rsqrt(jnp.sum(qraw * qraw, axis=1, keepdims=True) + epsilon)

    def right(s):
        b = (z + 8 - s) % 8
        return push(qall.at[b], qall.at[b], ring_sem, s, at(0, 1, 0))

    def left(s):
        b = (z + s) % 8
        return push(qall.at[b], qall.at[b], ring_sem, 4 + s, at(0, 7, 0))

    def ring(s):
        if s:
            right(s - 1).wait_recv()
            if s < 4:
                left(s - 1).wait_recv()
        right(s).start()
        if s < 3:
            left(s).start()

    ring(0)

    inncat[...] = lhs(jnp.transpose(inner_ref[...]))
    outcat[...] = lhs(jnp.transpose(outer_ref[...]))

    def rows(t, carry):
        r = pl.ds(pl.multiple_of(t * 256, 256), 256)
        hid = dot(inncat[...], rhs(table_ref[r, :], 1), NT)
        h, l = split(dot(outcat[...], rhs(gelu(hid), 0)))
        zcat[0:256, r] = h
        zcat[256:512, r] = l
        return carry

    lax.fori_loop(0, 8, rows, 0, unroll=2)
    ring(1)

    for c in refs_cp:
        c.wait_recv()

    def piece(s):
        k = s // 2
        dx = (1 - k // 2) * (2 + k) + (k // 2) * (3 - k)
        dy = 1 - s % 2
        return pbdev(dy, dx)

    def part_cp(s):
        return push(part.at[s], got.at[p], part_sem, s, piece(s))

    def pieces(s, carry):
        b = piece(s)[0]
        refs = refs_all[b]
        slot = lax.broadcasted_iota(jnp.int32, (CAP, 256), 0) + p * CAP
        uses = jnp.zeros((CAP, 256), f32)
        for k in range(8):
            uses = uses + jnp.where(slot == refs[k : k + 1, :], 1.0, 0.0)
        uses = uses.astype(bf16)
        listed = lists_ref[pl.ds(b, 1), :]
        for t in range(2):
            row = lax.broadcasted_iota(jnp.int32, (1024, CAP), 0) + t * 1024
            pick = jnp.where(row == listed, 1.0, 0.0).astype(bf16)
            ct[b, t * 1024 : (t + 1) * 1024, :] = dot(pick, uses).astype(bf16)
        total = dot(zcat[...], ct[b])
        total = total[0:256] + total[256:512]

        @pl.when(s < 7)
        def _():
            part[s] = total
            part_cp(s).start()

        @pl.when(s == 7)
        def _():
            got[p] = total

        return carry

    lax.fori_loop(0, 4, pieces, 0)
    ring(2)
    lax.fori_loop(4, 8, pieces, 0)
    ring(3)
    right(3).wait_recv()

    def queries(b, carry):
        q = qall[b]
        qn[b] = rhs(q, 1)
        qr[b] = rhs(q, 0)
        return carry

    lax.fori_loop(0, 8, queries, 0)
    for s in range(7):
        part_cp(s).wait_recv()
    raw = got[0]
    for b in range(1, 8):
        raw = raw + got[b]
    raw = jnp.transpose(raw)
    inv_norm = lax.rsqrt(jnp.sum(raw * raw, axis=1, keepdims=True) + epsilon)
    items[0] = raw * inv_norm

    item_cp = [
        push(items.at[0], items.at[2], item_sem, 1, at(1, 0, 0)),
        push(items.at[0], items.at[1], item_sem, 0, at(0, 0, 1)),
        push(items.at[2], items.at[3], item_sem, 2, at(0, 0, 1)),
    ]
    item_cp[0].start()
    item_cp[1].start()
    stats[...] = jnp.zeros((16, 256), f32)

    def numbers(i):
        row = lax.broadcasted_iota(jnp.int32, (512, 256), 0)
        a = ((yh + i) % 2) * 16 + z * 2
        first, second = (a + core) * 256, (a + 1 - core) * 256 - 256
        return row + jnp.where(row < 256, first, second)

    def logits(i):
        here = lhs(items[2 * i : 2 * i + 2].reshape(512, 256))
        number = numbers(i)

        def step(b, carry):
            lg = inverse_temp * dot(here, qn[b], NT)
            e = jnp.exp(lg)
            ex[i, b] = e
            r = pl.ds(b, 1)
            stats[r, :] = stats[r, :] + jnp.sum(e, axis=0, keepdims=True)
            hit = pos_all[b][0:1, :] == number
            r8 = pl.ds(b + 8, 1)
            stats[r8, :] = stats[r8, :] + jnp.sum(jnp.where(hit, lg, 0.0), axis=0, keepdims=True)
            return carry

        lax.fori_loop(0, 8, step, 0)

    for c in pos_cp:
        c.wait_recv()
    item_cp[1].wait_recv()
    logits(0)
    item_cp[0].wait_recv()
    item_cp[2].start()
    item_cp[2].wait_recv()
    logits(1)

    stat_cp = [push(stats, stats_all.at[z], stat_sem, i, at(0, i + 1, 0)) for i in range(7)]
    for c in stat_cp:
        c.start()
    stats_all[z] = stats[...]
    for i in range(2):
        h, l = split(jnp.transpose(items[2 * i : 2 * i + 2].reshape(512, 256)))
        tcat[i] = jnp.concatenate([h, l, h], axis=1)
    for c in stat_cp:
        c.wait()
    both = stats_all[0]
    for b in range(1, 8):
        both = both + stats_all[b]
    stats[...] = both
    loss_ref[...] = jnp.log(stats[pl.ds(z, 1), :]) - stats[pl.ds(z + 8, 1), :]
    stats[0:8, :] = inverse_temp / both[0:8, :]

    def coefficients(i, b):
        hit = pos_all[b][0:1, :] == numbers(i)
        return split(ex[i, b] * stats[pl.ds(b, 1), :] - jnp.where(hit, inverse_temp, 0.0))

    def item_part(c, b):
        return dot(jnp.concatenate([c[0], c[0], c[1]], axis=1), qr[b])

    def far_items(b, total):
        return total + item_part(coefficients(1, b), b)

    total = lax.fori_loop(0, 8, far_items, jnp.zeros((512, 256), f32))
    to_sib = [push(dsend.at[i], dgot.at[i], near_sem, i, at(0, 0, 1)) for i in range(2)]
    across = push(dsend.at[2], dgot.at[2], near_sem, 2, at(1, 0, 0))
    dsend[0] = total[256:512]
    to_sib[0].start()
    dsend[2] = total[0:256]

    def both_sides(b, total):
        c0, c1 = coefficients(0, b), coefficients(1, b)
        dq[b] = dot(tcat[0], jnp.concatenate([c0[0], c0[0], c0[1]], axis=0)) + dot(
            tcat[1], jnp.concatenate([c1[0], c1[0], c1[1]], axis=0)
        )
        return total + item_part(c0, b)

    def blocks(s, total):
        return both_sides((z + 5 + s) % 8, both_sides((z + 4 - s) % 8, total))

    def q_right(s):
        return push(qsend.at[s], qgot.at[s], q_sem, s, at(0, 1, 0))

    def q_left(s):
        return push(qsend.at[4 + s], qgot.at[4 + s], q_sem, 4 + s, at(0, 7, 0))

    def q_step(s):
        mine = dq[(z + 4 - s) % 8]
        if s:
            q_right(s - 1).wait_recv()
            mine = mine + qgot[s - 1]
        qsend[s] = mine
        q_right(s).start()
        if s < 3:
            mine = dq[(z + 5 + s) % 8]
            if s:
                q_left(s - 1).wait_recv()
                mine = mine + qgot[4 + s - 1]
            qsend[4 + s] = mine
            q_left(s).start()

    total = blocks(0, jnp.zeros((512, 256), f32))
    to_sib[0].wait_recv()
    dsend[2] = dsend[2] + dgot[0]
    across.start()
    q_step(0)
    total = lax.fori_loop(1, 4, blocks, total)
    dsend[1] = total[256:512]
    to_sib[1].start()
    q_step(1)
    to_sib[1].wait_recv()
    mine = total[0:256] + dgot[1]
    across.wait_recv()
    d = mine + dgot[2]
    emb = items[0]
    d = inv_norm * (d - emb * jnp.sum(emb * d, axis=1, keepdims=True))

    for h in range(2):
        draw[h] = d[:, h * 128 : (h + 1) * 128]
        d_all[h, p] = d[:, h * 128 : (h + 1) * 128]

    def d_cp(h, i):
        return push(draw.at[h], d_all.at[h, p], d_sem, h * 7 + i, pbdev(*order[i]))

    for h in range(2):
        for i in range(7):
            d_cp(h, i).start()

    def add_rows(h, b, first):
        dcat = jnp.concatenate(split(d_all[h, b]), axis=1)
        for a in range(2):
            r = dot(ct[b, a * 1024 : (a + 1) * 1024, :], dcat)
            r = (r[:, 0:128] + r[:, 128:256]).reshape(8, 2, 64, 128)
            acc[h, a] = r if first else acc[h, a] + r

    def c_cp(h):
        return push(acc.at[h, :, :, 1 - core], cgot.at[h], c_sem, h, at(0, 0, 1))

    def z_right(h, s):
        return push(zsend.at[h, s], zgot.at[h, s], z_sem, h * 7 + s, at(0, 1, 0))

    def z_left(h, s):
        return push(zsend.at[h, 4 + s], zgot.at[h, 4 + s], z_sem, h * 7 + 4 + s, at(0, 7, 0))

    def rows_of(h, d):
        return acc[h, :, (z + d) % 8, core] + cgot[h, :, (z + d) % 8]

    def z_step(h, s):
        v = rows_of(h, 4 - s)
        if s:
            z_right(h, s - 1).wait_recv()
            v = v + zgot[h, s - 1]
        zsend[h, s] = v
        z_right(h, s).start()
        if s < 3:
            v = rows_of(h, 5 + s)
            if s:
                z_left(h, s - 1).wait_recv()
                v = v + zgot[h, 4 + s - 1]
            zsend[h, 4 + s] = v
            z_left(h, s).start()

    add_rows(0, p, True)
    add_rows(1, p, True)
    for i in range(7):
        if i == 3:
            q_step(2)
        d_cp(0, i).wait_recv()
        add_rows(0, pb_from[i], False)
    c_cp(0).start()
    q_step(3)
    c_cp(0).wait_recv()
    z_step(0, 0)
    for i in range(7):
        d_cp(1, i).wait_recv()
        add_rows(1, pb_from[i], False)
        if i in (1, 3, 5):
            z_step(0, (i + 1) // 2)
    c_cp(1).start()

    y_cp = [push(ysend.at[h], ygot.at[h], y_sem, h, at(1, 0, 0)) for h in range(2)]

    def to_y(h):
        z_left(h, 2).wait_recv()
        z_right(h, 3).wait_recv()
        v = rows_of(h, 0) + (zgot[h, 3] + zgot[h, 6])
        zgot[h, 0] = v
        ysend[h] = zgot[h, 0, 1 - yh]
        y_cp[h].start()

    c_cp(1).wait_recv()
    z_step(1, 0)
    to_y(0)
    q_right(3).wait_recv()
    q_left(2).wait_recv()
    d = jnp.transpose(dq[z] + (qgot[3] + qgot[6]))
    qraw = qraw_s[...]
    inv_norm = lax.rsqrt(jnp.sum(qraw * qraw, axis=1, keepdims=True) + epsilon)
    emb = qraw * inv_norm
    d = inv_norm * (d - emb * jnp.sum(emb * d, axis=1, keepdims=True))
    d = dot3(d, qo_ref[...], NT) * gelu_slope(qpre_s[...])
    z_step(1, 1)
    qg_ref[...] = dot3(d, qi_ref[...], NT)
    z_step(1, 2)
    own = table_ref[pl.ds(pl.multiple_of(j * 64, 64), 64), :]
    slope = gelu_slope(dot3(own, inner_ref[...]))
    z_step(1, 3)
    to_y(1)
    y_cp[0].wait_recv()
    y_cp[1].wait_recv()
    v = jnp.concatenate([zgot[h, 0, yh] + ygot[h] for h in range(2)], axis=1)
    d = dot3(v, outer_ref[...], NT) * slope
    tg_ref[...] = dot3(d, inner_ref[...], NT)

    for c in refs_cp + pos_cp + item_cp + to_sib + [across] + y_cp:
        c.wait_send()
    for s in range(4):
        right(s).wait_send()
        q_right(s).wait_send()
    for s in range(3):
        left(s).wait_send()
        q_left(s).wait_send()
    for s in range(7):
        part_cp(s).wait_send()
    for h in range(2):
        c_cp(h).wait_send()
        for i in range(7):
            d_cp(h, i).wait_send()
        for s in range(4):
            z_right(h, s).wait_send()
        for s in range(3):
            z_left(h, s).wait_send()


def per_device(
    query_feats,
    item_table,
    serve_ids,
    block_counts,
    item_refs,
    positive,
    query_inner,
    query_outer,
    item_inner,
    item_outer,
):
    vm = pl.BlockSpec(memory_space=pltpu.VMEM)
    sm = pl.BlockSpec(memory_space=pltpu.SMEM)
    loss, query_grad, table_grad = pl.pallas_call(
        step_kernel,
        name="step",
        out_shape=[
            jax.ShapeDtypeStruct((1, 256), f32),
            jax.ShapeDtypeStruct((256, 256), f32),
            jax.ShapeDtypeStruct((64, 256), f32),
        ],
        in_specs=[vm, sm] + [vm] * 8,
        out_specs=[vm] * 3,
        scratch_shapes=[
            VM((8, 256), jnp.int32),
            VM((8, 8, 256), jnp.int32),
            VM((8, 256), jnp.int32),
            VM((8, 8, 256), jnp.int32),
            VM((512, 2048), bf16),
            VM((512, 768), bf16),
            VM((256, 1536), bf16),
            VM((8, 256, 256), f32),
            VM((256, 512), f32),
            VM((256, 256), f32),
            VM((8, 2048, 256), bf16),
            VM((7, 256, 256), f32),
            VM((8, 256, 256), f32),
            VM((4, 256, 256), f32),
            VM((8, 256, 768), bf16),
            VM((8, 768, 256), bf16),
            VM((2, 256, 1536), bf16),
            VM((2, 8, 512, 256), f32),
            VM((16, 256), f32),
            VM((8, 16, 256), f32),
            VM((3, 256, 256), f32),
            VM((3, 256, 256), f32),
            VM((2, 256, 128), f32),
            VM((2, 8, 256, 128), f32),
            VM((8, 256, 256), f32),
            VM((2, 2, 8, 2, 64, 128), f32),
            VM((2, 2, 8, 64, 128), f32),
            VM((2, 7, 2, 64, 128), f32),
            VM((2, 7, 2, 64, 128), f32),
            VM((2, 64, 128), f32),
            VM((2, 64, 128), f32),
            VM((7, 256, 256), f32),
            VM((7, 256, 256), f32),
            DMA((2, 7)),
            DMA((2, 7)),
            DMA((2, 7)),
            DMA((2, 7)),
            DMA((2, 3)),
            DMA((2, 7)),
            DMA((2, 3)),
            DMA((2, 14)),
            DMA((2, 2)),
            DMA((2, 14)),
            DMA((2, 2)),
            DMA((2, 7)),
        ],
        compiler_params=pltpu.CompilerParams(
            collective_id=1, has_side_effects=True, vmem_limit_bytes=60 << 20
        ),
    )(
        item_refs.T,
        block_counts[0, 0],
        serve_ids[0, 0],
        positive.reshape(1, 256),
        item_table,
        item_inner,
        item_outer,
        query_feats,
        query_inner,
        query_outer,
    )
    return (loss.reshape(256), query_grad, table_grad)


def solution(mesh):
    placed = (
        P(("pb", "ia"), None),
        P("pb", None),
        P("pb", "ia", None, None),
        P("pb", "ia", None),
        P(("pb", "ia"), None),
        P(("pb", "ia")),
        P(),
        P(),
        P(),
        P(),
    )
    return jax.shard_map(
        per_device,
        mesh=mesh,
        in_specs=placed,
        out_specs=(P(("pb", "ia")), P(("pb", "ia"), None), P(("pb", "ia"), None)),
        check_vma=False,
    )
```

```python
import jax
import jax.numpy as jnp
from jax import lax
from jax.experimental import pallas as pl
from jax.experimental.pallas import tpu as pltpu
from jax.sharding import PartitionSpec as P

BLOCK = 128
CAP = 512
MESH = pl.DeviceIdType.MESH
VM = pltpu.VMEM
DMA = pltpu.SemaphoreType.DMA
f32 = jnp.float32
bf16 = jnp.bfloat16

inverse_temp = 20.0
epsilon = 1e-06

NN = (((1,), (0,)), ((), ()))
NT = (((1,), (1,)), ((), ()))


def split(v):
    hi = v.astype(bf16)
    return hi, (v - hi.astype(f32)).astype(bf16)


def dot(a, b, dims=NN):
    return lax.dot_general(a, b, dims, preferred_element_type=f32)


def lhs(v):
    h, l = split(v)
    return jnp.concatenate([h, h, l], axis=1)


def rhs(v, axis):
    h, l = split(v)
    return jnp.concatenate([h, l, h], axis=axis)


def dot3(a, b, dims=NN):
    return dot(lhs(a), rhs(b, dims[0][1][0]), dims)


def normal_cdf(v):
    return 0.5 * (1.0 + lax.erf(v * 0.7071067811865476))


def gelu(v):
    return v * normal_cdf(v)


def gelu_slope(v):
    return normal_cdf(v) + v * (0.3989422804014327 * jnp.exp(-0.5 * v * v))


def place():
    p, j = lax.axis_index("pb"), lax.axis_index("ia")
    return p, j, p % 4, p // 4, j // 16, (j // 2) % 8, j % 2


def greet(peers):
    barrier = pltpu.get_barrier_semaphore()
    for peer in peers:
        pl.semaphore_signal(barrier, inc=1, device_id=peer, device_id_type=MESH)
    pl.semaphore_wait(barrier, len(peers))


def push(src, dst, sems, k, peer):
    return pltpu.make_async_remote_copy(
        src_ref=src,
        dst_ref=dst,
        send_sem=sems.at[0, k],
        recv_sem=sems.at[1, k],
        device_id=peer,
        device_id_type=MESH,
    )


def step_kernel(
    refs_ref,
    counts_ref,
    lists_ref,
    pos_ref,
    table_hbm,
    inner_hbm,
    outer_hbm,
    qf_hbm,
    qi_hbm,
    qo_hbm,
    loss_ref,
    qg_ref,
    tg_ref,
    table_ref,
    inner_ref,
    outer_ref,
    qf_ref,
    qi_ref,
    qo_ref,
    live,
    refs_all,
    posb,
    pos_all,
    zcat,
    inncat,
    outcat,
    qall,
    qpre_s,
    qraw_s,
    ct,
    part,
    got,
    items,
    qn,
    qr,
    tcat,
    ex,
    stats,
    stats_all,
    dsend,
    dgot,
    draw,
    d_all,
    dq,
    acc,
    cgot,
    esum,
    egot,
    vcat,
    outr,
    innr,
    slope,
    qsend,
    qgot,
    load_sem,
    refs_sem,
    pos_sem,
    ring_sem,
    zt_sem,
    part_sem,
    item_sem,
    stat_sem,
    near_sem,
    d_sem,
    c_sem,
    e_sem,
    q_sem,
):
    p, j, x, yl, yh, z, core = place()
    loads = [
        pltpu.make_async_copy(src, dst, load_sem.at[i])
        for i, (src, dst) in enumerate(
            [
                (qf_hbm, qf_ref),
                (qi_hbm, qi_ref),
                (qo_hbm, qo_ref),
                (inner_hbm, inner_ref),
                (outer_hbm, outer_ref),
                (table_hbm, table_ref),
            ]
        )
    ]
    for c in loads:
        c.start()

    def at(dyh, dz, dc):
        return (p, (((yh + dyh) % 2) * 8 + (z + dz) % 8) * 2 + (core + dc) % 2)

    def pbdev(dy, dx):
        return (((yl + dy) % 2) * 4 + (x + dx) % 4, j)

    order = [(1, 0), (0, 1), (0, 3), (0, 2), (1, 1), (1, 3), (1, 2)]
    pb_from = [((yl + dy) % 2) * 4 + (x + 4 - dx) % 4 for dy, dx in order]
    others = [(a, d) for d in (4, 3, 5, 2, 6, 1, 7, 0) for a in (0, 1) if a or d]
    greet(
        [pbdev(*d) for d in order]
        + [at(a, d, 0) for a, d in others]
        + [at(0, 0, 1)]
    )

    refs = refs_ref[...]
    owner = refs // CAP
    limit = jnp.zeros((8, 256), jnp.int32)
    for o in range(8):
        limit = jnp.where(owner == o, BLOCK * counts_ref[o], limit)
    live[...] = jnp.where(refs - owner * CAP < limit, refs, -1)
    refs_all[p] = live[...]
    posb[...] = jnp.broadcast_to(pos_ref[...], (8, 256))
    pos_all[z] = posb[...]
    refs_cp = [push(live, refs_all.at[p], refs_sem, i, pbdev(*d)) for i, d in enumerate(order)]
    pos_cp = [push(posb, pos_all.at[z], pos_sem, i, at(0, i + 1, 0)) for i in range(7)]
    for c in refs_cp + pos_cp:
        c.start()

    for c in loads[:3]:
        c.wait()
    qpre = dot3(qf_ref[...], qi_ref[...])
    qpre_s[...] = qpre
    qraw = dot3(gelu(qpre), qo_ref[...])
    qraw_s[...] = qraw
    qall[z] = qraw * lax.rsqrt(jnp.sum(qraw * qraw, axis=1, keepdims=True) + epsilon)

    def right(s):
        b = (z + 8 - s) % 8
        return push(qall.at[b], qall.at[b], ring_sem, s, at(0, 1, 0))

    def left(s):
        b = (z + s) % 8
        return push(qall.at[b], qall.at[b], ring_sem, 4 + s, at(0, 7, 0))

    def ring(s):
        if s:
            right(s - 1).wait_recv()
            if s < 4:
                left(s - 1).wait_recv()
        right(s).start()
        if s < 3:
            left(s).start()

    ring(0)

    for c in loads[3:]:
        c.wait()
    inncat[...] = lhs(jnp.transpose(inner_ref[...]))
    outcat[...] = lhs(jnp.transpose(outer_ref[...]))

    def share(i):
        t = core * 4 + i
        return push(dq.at[t], dq.at[t], zt_sem, i, at(0, 0, 1))

    def keep(t):
        r = pl.ds(pl.multiple_of(t * 256, 256), 256)
        h, l = split(dq[t])
        zcat[0:256, r] = h
        zcat[256:512, r] = l

    def rows(i, carry):
        t = core * 4 + i
        r = pl.ds(pl.multiple_of(t * 256, 256), 256)
        hid = dot(inncat[...], rhs(table_ref[r, :], 1), NT)
        dq[t] = dot(outcat[...], rhs(gelu(hid), 0))
        share(i).start()
        keep(t)
        return carry

    lax.fori_loop(0, 4, rows, 0, unroll=2)
    ring(1)
    for i in range(4):
        share(i).wait_recv()
        keep((1 - core) * 4 + i)
    for i in range(4):
        share(i).wait_send()

    for c in refs_cp:
        c.wait_recv()

    def piece(s):
        k = s // 2
        dx = (1 - k // 2) * (2 + k) + (k // 2) * (3 - k)
        dy = 1 - s % 2
        return pbdev(dy, dx)

    def part_cp(s):
        return push(part.at[s], got.at[p], part_sem, s, piece(s))

    def pieces(s, carry):
        b = piece(s)[0]
        refs = refs_all[b]
        slot = lax.broadcasted_iota(jnp.int32, (CAP, 256), 0) + p * CAP
        uses = jnp.zeros((CAP, 256), f32)
        for k in range(8):
            uses = uses + jnp.where(slot == refs[k : k + 1, :], 1.0, 0.0)
        uses = uses.astype(bf16)
        listed = lists_ref[pl.ds(b, 1), :]
        for t in range(2):
            row = lax.broadcasted_iota(jnp.int32, (1024, CAP), 0) + t * 1024
            pick = jnp.where(row == listed, 1.0, 0.0).astype(bf16)
            ct[b, t * 1024 : (t + 1) * 1024, :] = dot(pick, uses).astype(bf16)
        total = dot(zcat[...], ct[b])
        total = total[0:256] + total[256:512]

        @pl.when(s < 7)
        def _():
            part[s] = total
            part_cp(s).start()

        @pl.when(s == 7)
        def _():
            got[p] = total

        return carry

    lax.fori_loop(0, 4, pieces, 0)
    ring(2)
    lax.fori_loop(4, 8, pieces, 0)
    ring(3)
    right(3).wait_recv()

    def queries(b, carry):
        q = qall[b]
        qn[b] = rhs(q, 1)
        qr[b] = rhs(q, 0)
        return carry

    lax.fori_loop(0, 8, queries, 0)
    for s in range(7):
        part_cp(s).wait_recv()
    raw = got[0]
    for b in range(1, 8):
        raw = raw + got[b]
    raw = jnp.transpose(raw)
    inv_norm = lax.rsqrt(jnp.sum(raw * raw, axis=1, keepdims=True) + epsilon)
    items[0] = raw * inv_norm

    item_cp = [
        push(items.at[0], items.at[2], item_sem, 1, at(1, 0, 0)),
        push(items.at[0], items.at[1], item_sem, 0, at(0, 0, 1)),
        push(items.at[2], items.at[3], item_sem, 2, at(0, 0, 1)),
    ]
    item_cp[0].start()
    item_cp[1].start()
    stats[...] = jnp.zeros((16, 256), f32)

    def numbers(i):
        row = lax.broadcasted_iota(jnp.int32, (512, 256), 0)
        a = ((yh + i) % 2) * 16 + z * 2
        first, second = (a + core) * 256, (a + 1 - core) * 256 - 256
        return row + jnp.where(row < 256, first, second)

    def logits(i, first, last):
        if last - first == 512:
            here = lhs(items[2 * i : 2 * i + 2].reshape(512, 256))
        else:
            here = lhs(items[2 * i + first // 256])
        number = numbers(i)[first:last]

        def step(b, carry):
            lg = inverse_temp * dot(here, qn[b], NT)
            e = jnp.exp(lg)
            ex[i, b, first:last] = e
            r = pl.ds(b, 1)
            stats[r, :] = stats[r, :] + jnp.sum(e, axis=0, keepdims=True)
            hit = pos_all[b][0:1, :] == number
            r8 = pl.ds(b + 8, 1)
            stats[r8, :] = stats[r8, :] + jnp.sum(jnp.where(hit, lg, 0.0), axis=0, keepdims=True)
            return carry

        lax.fori_loop(0, 8, step, 0)

    for c in pos_cp:
        c.wait_recv()
    item_cp[1].wait_recv()
    logits(0, 0, 512)
    item_cp[0].wait_recv()
    item_cp[2].start()
    logits(1, 0, 256)
    item_cp[2].wait_recv()
    logits(1, 256, 512)

    stat_cp = [push(stats, stats_all.at[z], stat_sem, i, at(0, i + 1, 0)) for i in range(7)]
    for c in stat_cp:
        c.start()
    stats_all[z] = stats[...]
    for i in range(2):
        h, l = split(jnp.transpose(items[2 * i : 2 * i + 2].reshape(512, 256)))
        tcat[i] = jnp.concatenate([h, l, h], axis=1)
    outr[...] = rhs(outer_ref[...], 1)
    innr[...] = rhs(inner_ref[...], 1)
    own = table_ref[pl.ds(pl.multiple_of(j * 64, 64), 64), :]
    slope[...] = gelu_slope(dot3(own, inner_ref[...]))
    for c in stat_cp:
        c.wait()
    both = stats_all[0]
    for b in range(1, 8):
        both = both + stats_all[b]
    stats[...] = both
    loss = jnp.log(stats[pl.ds(z, 1), :]) - stats[pl.ds(z + 8, 1), :]
    loss_ref[...] = loss.reshape(256)
    stats[0:8, :] = inverse_temp / both[0:8, :]

    def coefficients(i, b):
        hit = pos_all[b][0:1, :] == numbers(i)
        return split(ex[i, b] * stats[pl.ds(b, 1), :] - jnp.where(hit, inverse_temp, 0.0))

    def item_part(c, b):
        return dot(jnp.concatenate([c[0], c[0], c[1]], axis=1), qr[b])

    def far_items(first):
        def step(b, total):
            hit = pos_all[b][0:1, :] == numbers(1)[first : first + 256]
            c = ex[1, b, first : first + 256] * stats[pl.ds(b, 1), :]
            return total + item_part(split(c - jnp.where(hit, inverse_temp, 0.0)), b)

        return lax.fori_loop(0, 8, step, jnp.zeros((256, 256), f32), unroll=2)

    to_sib = [push(dsend.at[i], dgot.at[i], near_sem, i, at(0, 0, 1)) for i in range(2)]
    across = push(dsend.at[2], dgot.at[2], near_sem, 2, at(1, 0, 0))
    dsend[0] = far_items(256)
    to_sib[0].start()
    total = far_items(0)
    to_sib[0].wait_recv()
    dsend[2] = total + dgot[0]
    across.start()

    def both_sides(b, total):
        c0, c1 = coefficients(0, b), coefficients(1, b)
        dq[b] = dot(tcat[0], jnp.concatenate([c0[0], c0[0], c0[1]], axis=0)) + dot(
            tcat[1], jnp.concatenate([c1[0], c1[0], c1[1]], axis=0)
        )
        return total + item_part(c0, b)

    def blocks(s, total):
        return both_sides((z + 5 + s) % 8, both_sides((z + 4 - s) % 8, total))

    def q_right(s):
        return push(qsend.at[s], qgot.at[s], q_sem, s, at(0, 1, 0))

    def q_left(s):
        return push(qsend.at[4 + s], qgot.at[4 + s], q_sem, 4 + s, at(0, 7, 0))

    def q_step(s):
        mine = dq[(z + 4 - s) % 8]
        if s:
            q_right(s - 1).wait_recv()
            mine = mine + qgot[s - 1]
        qsend[s] = mine
        q_right(s).start()
        if s < 3:
            mine = dq[(z + 5 + s) % 8]
            if s:
                q_left(s - 1).wait_recv()
                mine = mine + qgot[4 + s - 1]
            qsend[4 + s] = mine
            q_left(s).start()

    total = blocks(0, jnp.zeros((512, 256), f32))
    q_step(0)
    total = lax.fori_loop(1, 4, blocks, total)
    dsend[1] = total[256:512]
    to_sib[1].start()
    q_step(1)
    to_sib[1].wait_recv()
    mine = total[0:256] + dgot[1]
    across.wait_recv()
    d = mine + dgot[2]
    emb = items[0]
    d = inv_norm * (d - emb * jnp.sum(emb * d, axis=1, keepdims=True))

    for h in range(2):
        draw[h] = d[:, h * 128 : (h + 1) * 128]
        d_all[h, p] = d[:, h * 128 : (h + 1) * 128]

    def d_cp(h, i):
        return push(draw.at[h], d_all.at[h, p], d_sem, h * 7 + i, pbdev(*order[i]))

    for h in range(2):
        for i in range(7):
            d_cp(h, i).start()

    def add_rows(h, b, first):
        dcat = jnp.concatenate(split(d_all[h, b]), axis=1)
        for a in range(2):
            r = dot(ct[b, a * 1024 : (a + 1) * 1024, :], dcat)
            r = (r[:, 0:128] + r[:, 128:256]).reshape(8, 2, 64, 128)
            acc[h, a] = r if first else acc[h, a] + r

    def c_cp(h):
        return push(acc.at[h, :, :, 1 - core], cgot.at[h], c_sem, h, at(0, 0, 1))

    def e_cp(h, k):
        a, d = others[k]
        src = esum.at[h, (yh + a) % 2, (z + d) % 8]
        return push(src, egot.at[h, k], e_sem, h * 15 + k, at(a, d, 0))

    def send_rows(h):
        c_cp(h).wait_recv()
        esum[h] = acc[h, :, :, core] + cgot[h]
        for k in range(15):
            e_cp(h, k).start()

    add_rows(0, p, True)
    add_rows(1, p, True)
    for i in range(7):
        if i == 2:
            q_step(2)
        d_cp(0, i).wait_recv()
        add_rows(0, pb_from[i], False)
    c_cp(0).start()
    q_step(3)
    send_rows(0)
    for i in range(7):
        d_cp(1, i).wait_recv()
        add_rows(1, pb_from[i], False)
    c_cp(1).start()
    send_rows(1)
    q_right(3).wait_recv()
    q_left(2).wait_recv()
    d = jnp.transpose(dq[z] + (qgot[3] + qgot[6]))
    qraw = qraw_s[...]
    inv_norm = lax.rsqrt(jnp.sum(qraw * qraw, axis=1, keepdims=True) + epsilon)
    emb = qraw * inv_norm
    d = inv_norm * (d - emb * jnp.sum(emb * d, axis=1, keepdims=True))
    d = dot3(d, qo_ref[...], NT) * gelu_slope(qpre_s[...])
    qg_ref[...] = dot3(d, qi_ref[...], NT)
    for h in range(2):
        for k in range(15):
            e_cp(h, k).wait_recv()
        v = esum[h, yh, z]
        for k in range(15):
            v = v + egot[h, k]
        vcat[:, h * 128 : (h + 1) * 128] = v
    d = dot(lhs(vcat[...]), outr[...], NT) * slope[...]
    tg_ref[...] = dot(lhs(d), innr[...], NT)

    for c in refs_cp + pos_cp + item_cp + to_sib + [across]:
        c.wait_send()
    for s in range(4):
        right(s).wait_send()
        q_right(s).wait_send()
    for s in range(3):
        left(s).wait_send()
        q_left(s).wait_send()
    for s in range(7):
        part_cp(s).wait_send()
    for h in range(2):
        c_cp(h).wait_send()
        for i in range(7):
            d_cp(h, i).wait_send()
        for k in range(15):
            e_cp(h, k).wait_send()


def keep_kernel(a_ref, b_ref, c_ref, a_out, b_out, c_out):
    a_out[...] = a_ref[...]
    b_out[...] = b_ref[...]
    c_out[...] = c_ref[...]


def per_device(
    query_feats,
    item_table,
    serve_ids,
    block_counts,
    item_refs,
    positive,
    query_inner,
    query_outer,
    item_inner,
    item_outer,
):
    vm = pl.BlockSpec(memory_space=pltpu.VMEM)
    sm = pl.BlockSpec(memory_space=pltpu.SMEM)
    hbm = pl.BlockSpec(memory_space=pl.ANY)
    loss, query_grad, table_grad = pl.pallas_call(
        step_kernel,
        name="step",
        out_shape=[
            jax.ShapeDtypeStruct((256,), f32),
            jax.ShapeDtypeStruct((256, 256), f32),
            jax.ShapeDtypeStruct((64, 256), f32),
        ],
        in_specs=[vm, sm, vm, vm] + [hbm] * 6,
        out_specs=[vm] * 3,
        scratch_shapes=[
            VM((2048, 256), f32),
            VM((256, 512), f32),
            VM((512, 256), f32),
            VM((256, 256), f32),
            VM((256, 512), f32),
            VM((512, 256), f32),
            VM((8, 256), jnp.int32),
            VM((8, 8, 256), jnp.int32),
            VM((8, 256), jnp.int32),
            VM((8, 8, 256), jnp.int32),
            VM((512, 2048), bf16),
            VM((512, 768), bf16),
            VM((256, 1536), bf16),
            VM((8, 256, 256), f32),
            VM((256, 512), f32),
            VM((256, 256), f32),
            VM((8, 2048, 256), bf16),
            VM((7, 256, 256), f32),
            VM((8, 256, 256), f32),
            VM((4, 256, 256), f32),
            VM((8, 256, 768), bf16),
            VM((8, 768, 256), bf16),
            VM((2, 256, 1536), bf16),
            VM((2, 8, 512, 256), f32),
            VM((16, 256), f32),
            VM((8, 16, 256), f32),
            VM((3, 256, 256), f32),
            VM((3, 256, 256), f32),
            VM((2, 256, 128), f32),
            VM((2, 8, 256, 128), f32),
            VM((8, 256, 256), f32),
            VM((2, 2, 8, 2, 64, 128), f32),
            VM((2, 2, 8, 64, 128), f32),
            VM((2, 2, 8, 64, 128), f32),
            VM((2, 15, 64, 128), f32),
            VM((64, 256), f32),
            VM((512, 768), bf16),
            VM((256, 1536), bf16),
            VM((64, 512), f32),
            VM((7, 256, 256), f32),
            VM((7, 256, 256), f32),
            DMA((6,)),
            DMA((2, 7)),
            DMA((2, 7)),
            DMA((2, 7)),
            DMA((2, 4)),
            DMA((2, 7)),
            DMA((2, 3)),
            DMA((2, 7)),
            DMA((2, 3)),
            DMA((2, 14)),
            DMA((2, 2)),
            DMA((2, 30)),
            DMA((2, 7)),
        ],
        compiler_params=pltpu.CompilerParams(
            collective_id=1, has_side_effects=True, vmem_limit_bytes=60 << 20
        ),
    )(
        item_refs.T,
        block_counts[0, 0],
        serve_ids[0, 0],
        positive.reshape(1, 256),
        item_table,
        item_inner,
        item_outer,
        query_feats,
        query_inner,
        query_outer,
    )
    return pl.pallas_call(
        keep_kernel,
        name="keep",
        out_shape=[
            jax.ShapeDtypeStruct((256,), f32),
            jax.ShapeDtypeStruct((256, 256), f32),
            jax.ShapeDtypeStruct((64, 256), f32),
        ],
        in_specs=[vm] * 3,
        out_specs=[vm] * 3,
    )(loss, query_grad, table_grad)


def solution(mesh):
    placed = (
        P(("pb", "ia"), None),
        P("pb", None),
        P("pb", "ia", None, None),
        P("pb", "ia", None),
        P(("pb", "ia"), None),
        P(("pb", "ia")),
        P(),
        P(),
        P(),
        P(),
    )
    return jax.shard_map(
        per_device,
        mesh=mesh,
        in_specs=placed,
        out_specs=(P(("pb", "ia")), P(("pb", "ia"), None), P(("pb", "ia"), None)),
        check_vma=False,
    )
```

```python
import jax
import jax.numpy as jnp
from jax import lax
from jax.experimental import pallas as pl
from jax.experimental.pallas import tpu as pltpu
from jax.sharding import PartitionSpec as P

BLOCK = 128
CAP = 512
MESH = pl.DeviceIdType.MESH
VM = pltpu.VMEM
DMA = pltpu.SemaphoreType.DMA
f32 = jnp.float32
bf16 = jnp.bfloat16

inverse_temp = 20.0
epsilon = 1e-06

NN = (((1,), (0,)), ((), ()))
NT = (((1,), (1,)), ((), ()))


def split(v):
    hi = v.astype(bf16)
    return hi, (v - hi.astype(f32)).astype(bf16)


def dot(a, b, dims=NN):
    return lax.dot_general(a, b, dims, preferred_element_type=f32)


def lhs(v):
    h, l = split(v)
    return jnp.concatenate([h, h, l], axis=1)


def rhs(v, axis):
    h, l = split(v)
    return jnp.concatenate([h, l, h], axis=axis)


def dot3(a, b, dims=NN):
    return dot(lhs(a), rhs(b, dims[0][1][0]), dims)


def normal_cdf(v):
    return 0.5 * (1.0 + lax.erf(v * 0.7071067811865476))


def gelu(v):
    return v * normal_cdf(v)


def gelu_slope(v):
    return normal_cdf(v) + v * (0.3989422804014327 * jnp.exp(-0.5 * v * v))


def place():
    p, j = lax.axis_index("pb"), lax.axis_index("ia")
    return p, j, p % 4, p // 4, j // 16, (j // 2) % 8, j % 2


def greet(peers):
    barrier = pltpu.get_barrier_semaphore()
    for peer in peers:
        pl.semaphore_signal(barrier, inc=1, device_id=peer, device_id_type=MESH)
    pl.semaphore_wait(barrier, len(peers))


def push(src, dst, sems, k, peer):
    return pltpu.make_async_remote_copy(
        src_ref=src,
        dst_ref=dst,
        send_sem=sems.at[0, k],
        recv_sem=sems.at[1, k],
        device_id=peer,
        device_id_type=MESH,
    )


def step_kernel(
    refs_ref,
    counts_ref,
    lists_ref,
    pos_ref,
    table_hbm,
    inner_hbm,
    outer_hbm,
    qf_hbm,
    qi_hbm,
    qo_hbm,
    loss_ref,
    qg_ref,
    tg_ref,
    table_ref,
    inner_ref,
    outer_ref,
    qf_ref,
    qi_ref,
    qo_ref,
    live,
    refs_all,
    posb,
    pos_all,
    zcat,
    inncat,
    outcat,
    qall,
    qpre_s,
    qraw_s,
    ct,
    part,
    got,
    items,
    qn,
    qr,
    tcat,
    ex,
    stats,
    stats_all,
    dsend,
    dgot,
    draw,
    d_all,
    dq,
    acc,
    cgot,
    esum,
    egot,
    vcat,
    outr,
    innr,
    slope,
    qsend,
    qgot,
    load_sem,
    refs_sem,
    pos_sem,
    ring_sem,
    zt_sem,
    part_sem,
    item_sem,
    stat_sem,
    near_sem,
    d_sem,
    c_sem,
    e_sem,
    q_sem,
):
    p, j, x, yl, yh, z, core = place()
    loads = [
        pltpu.make_async_copy(src, dst, load_sem.at[i])
        for i, (src, dst) in enumerate(
            [
                (qf_hbm, qf_ref),
                (qi_hbm, qi_ref),
                (qo_hbm, qo_ref),
                (inner_hbm, inner_ref),
                (outer_hbm, outer_ref),
                (table_hbm, table_ref),
            ]
        )
    ]
    for c in loads:
        c.start()

    def at(dyh, dz, dc):
        return (p, (((yh + dyh) % 2) * 8 + (z + dz) % 8) * 2 + (core + dc) % 2)

    def pbdev(dy, dx):
        return (((yl + dy) % 2) * 4 + (x + dx) % 4, j)

    order = [(1, 0), (0, 1), (0, 3), (0, 2), (1, 1), (1, 3), (1, 2)]
    pb_from = [((yl + dy) % 2) * 4 + (x + 4 - dx) % 4 for dy, dx in order]
    others = [(a, d) for d in (4, 3, 5, 2, 6, 1, 7, 0) for a in (0, 1) if a or d]
    greet(
        [pbdev(*d) for d in order]
        + [at(a, d, 0) for a, d in others]
        + [at(0, 0, 1)]
    )

    refs = refs_ref[...]
    owner = refs // CAP
    limit = jnp.zeros((8, 256), jnp.int32)
    for o in range(8):
        limit = jnp.where(owner == o, BLOCK * counts_ref[o], limit)
    live[...] = jnp.where(refs - owner * CAP < limit, refs, -1)
    refs_all[p] = live[...]
    posb[...] = jnp.broadcast_to(pos_ref[...], (8, 256))
    pos_all[z] = posb[...]
    refs_cp = [push(live, refs_all.at[p], refs_sem, i, pbdev(*d)) for i, d in enumerate(order)]
    pos_cp = [push(posb, pos_all.at[z], pos_sem, i, at(0, i + 1, 0)) for i in range(7)]
    for c in refs_cp + pos_cp:
        c.start()

    for c in loads[:3]:
        c.wait()
    qpre = dot3(qf_ref[...], qi_ref[...])
    qpre_s[...] = qpre
    qraw = dot3(gelu(qpre), qo_ref[...])
    qraw_s[...] = qraw
    qall[z] = qraw * lax.rsqrt(jnp.sum(qraw * qraw, axis=1, keepdims=True) + epsilon)

    def right(s):
        b = (z + 8 - s) % 8
        return push(qall.at[b], qall.at[b], ring_sem, s, at(0, 1, 0))

    def left(s):
        b = (z + s) % 8
        return push(qall.at[b], qall.at[b], ring_sem, 4 + s, at(0, 7, 0))

    def ring(s):
        if s:
            right(s - 1).wait_recv()
            if s < 4:
                left(s - 1).wait_recv()
        right(s).start()
        if s < 3:
            left(s).start()

    ring(0)

    for c in loads[3:]:
        c.wait()
    inncat[...] = lhs(jnp.transpose(inner_ref[...]))
    outcat[...] = lhs(jnp.transpose(outer_ref[...]))

    def share(i):
        t = core * 4 + i
        return push(dq.at[t], dq.at[t], zt_sem, i, at(0, 0, 1))

    def keep(t):
        r = pl.ds(pl.multiple_of(t * 256, 256), 256)
        h, l = split(dq[t])
        zcat[0:256, r] = h
        zcat[256:512, r] = l

    def rows(i, carry):
        t = core * 4 + i
        r = pl.ds(pl.multiple_of(t * 256, 256), 256)
        hid = dot(inncat[...], rhs(table_ref[r, :], 1), NT)
        dq[t] = dot(outcat[...], rhs(gelu(hid), 0))
        share(i).start()
        keep(t)
        return carry

    lax.fori_loop(0, 4, rows, 0, unroll=2)
    ring(1)
    for i in range(4):
        share(i).wait_recv()
        keep((1 - core) * 4 + i)
    for i in range(4):
        share(i).wait_send()

    for c in refs_cp:
        c.wait_recv()

    def piece(s):
        k = s // 2
        dx = (1 - k // 2) * (2 + k) + (k // 2) * (3 - k)
        dy = 1 - s % 2
        return pbdev(dy, dx)

    def part_cp(s):
        return push(part.at[s], got.at[p], part_sem, s, piece(s))

    def pieces(s, carry):
        b = piece(s)[0]
        refs = refs_all[b]
        slot = lax.broadcasted_iota(jnp.int32, (CAP, 256), 0) + p * CAP
        uses = jnp.zeros((CAP, 256), f32)
        for k in range(8):
            uses = uses + jnp.where(slot == refs[k : k + 1, :], 1.0, 0.0)
        uses = uses.astype(bf16)
        listed = lists_ref[pl.ds(b, 1), :]
        for t in range(2):
            row = lax.broadcasted_iota(jnp.int32, (1024, CAP), 0) + t * 1024
            pick = jnp.where(row == listed, 1.0, 0.0).astype(bf16)
            ct[b, t * 1024 : (t + 1) * 1024, :] = dot(pick, uses).astype(bf16)
        total = dot(zcat[...], ct[b])
        total = total[0:256] + total[256:512]

        @pl.when(s < 7)
        def _():
            part[s] = total
            part_cp(s).start()

        @pl.when(s == 7)
        def _():
            got[p] = total

        return carry

    lax.fori_loop(0, 4, pieces, 0)
    ring(2)
    lax.fori_loop(4, 8, pieces, 0)
    ring(3)
    right(3).wait_recv()

    def queries(b, carry):
        q = qall[b]
        qn[b] = rhs(q, 1)
        qr[b] = rhs(q, 0)
        return carry

    lax.fori_loop(0, 8, queries, 0)
    for s in range(7):
        part_cp(s).wait_recv()
    raw = got[0]
    for b in range(1, 8):
        raw = raw + got[b]
    raw = jnp.transpose(raw)
    inv_norm = lax.rsqrt(jnp.sum(raw * raw, axis=1, keepdims=True) + epsilon)
    items[0] = raw * inv_norm

    item_cp = [
        push(items.at[0], items.at[2], item_sem, 1, at(1, 0, 0)),
        push(items.at[0], items.at[1], item_sem, 0, at(0, 0, 1)),
        push(items.at[2], items.at[3], item_sem, 2, at(0, 0, 1)),
    ]
    item_cp[0].start()
    item_cp[1].start()
    stats[...] = jnp.zeros((16, 256), f32)

    def numbers(i):
        row = lax.broadcasted_iota(jnp.int32, (512, 256), 0)
        a = ((yh + i) % 2) * 16 + z * 2
        first, second = (a + core) * 256, (a + 1 - core) * 256 - 256
        return row + jnp.where(row < 256, first, second)

    def logits(i, first, last):
        if last - first == 512:
            here = lhs(items[2 * i : 2 * i + 2].reshape(512, 256))
        else:
            here = lhs(items[2 * i + first // 256])
        number = numbers(i)[first:last]

        def step(b, carry):
            lg = inverse_temp * dot(here, qn[b], NT)
            e = jnp.exp(lg)
            ex[i, b, first:last] = e
            r = pl.ds(b, 1)
            stats[r, :] = stats[r, :] + jnp.sum(e, axis=0, keepdims=True)
            hit = pos_all[b][0:1, :] == number
            r8 = pl.ds(b + 8, 1)
            stats[r8, :] = stats[r8, :] + jnp.sum(jnp.where(hit, lg, 0.0), axis=0, keepdims=True)
            return carry

        lax.fori_loop(0, 8, step, 0)

    for c in pos_cp:
        c.wait_recv()
    item_cp[1].wait_recv()
    logits(0, 0, 512)
    item_cp[0].wait_recv()
    item_cp[2].start()
    logits(1, 0, 256)
    item_cp[2].wait_recv()
    logits(1, 256, 512)

    stat_cp = [push(stats, stats_all.at[z], stat_sem, i, at(0, i + 1, 0)) for i in range(7)]
    for c in stat_cp:
        c.start()
    stats_all[z] = stats[...]
    for i in range(2):
        h, l = split(jnp.transpose(items[2 * i : 2 * i + 2].reshape(512, 256)))
        tcat[i] = jnp.concatenate([h, l, h], axis=1)
    outr[...] = rhs(outer_ref[...], 1)
    innr[...] = rhs(inner_ref[...], 1)
    own = table_ref[pl.ds(pl.multiple_of(j * 64, 64), 64), :]
    slope[...] = gelu_slope(dot3(own, inner_ref[...]))
    for c in stat_cp:
        c.wait()
    both = stats_all[0]
    for b in range(1, 8):
        both = both + stats_all[b]
    stats[...] = both
    loss = jnp.log(stats[pl.ds(z, 1), :]) - stats[pl.ds(z + 8, 1), :]
    loss_ref[...] = loss.reshape(256)
    stats[0:8, :] = inverse_temp / both[0:8, :]

    def coefficients(i, b):
        hit = pos_all[b][0:1, :] == numbers(i)
        return split(ex[i, b] * stats[pl.ds(b, 1), :] - jnp.where(hit, inverse_temp, 0.0))

    def item_part(c, b):
        return dot(jnp.concatenate([c[0], c[0], c[1]], axis=1), qr[b])

    def far_items(first):
        def step(b, total):
            hit = pos_all[b][0:1, :] == numbers(1)[first : first + 256]
            c = ex[1, b, first : first + 256] * stats[pl.ds(b, 1), :]
            return total + item_part(split(c - jnp.where(hit, inverse_temp, 0.0)), b)

        return lax.fori_loop(0, 8, step, jnp.zeros((256, 256), f32), unroll=2)

    to_sib = [push(dsend.at[i], dgot.at[i], near_sem, i, at(0, 0, 1)) for i in range(2)]
    across = push(dsend.at[2], dgot.at[2], near_sem, 2, at(1, 0, 0))
    dsend[0] = far_items(256)
    to_sib[0].start()
    total = far_items(0)
    to_sib[0].wait_recv()
    dsend[2] = total + dgot[0]
    across.start()

    def both_sides(b, total):
        c0, c1 = coefficients(0, b), coefficients(1, b)
        dq[b] = dot(tcat[0], jnp.concatenate([c0[0], c0[0], c0[1]], axis=0)) + dot(
            tcat[1], jnp.concatenate([c1[0], c1[0], c1[1]], axis=0)
        )
        return total + item_part(c0, b)

    def blocks(s, total):
        return both_sides((z + 5 + s) % 8, both_sides((z + 4 - s) % 8, total))

    def q_right(s, u):
        r = pl.ds(128 * u, 128)
        return push(qsend.at[s, r], qgot.at[s, r], q_sem, 2 * s + u, at(0, 1, 0))

    def q_left(s, u):
        r = pl.ds(128 * u, 128)
        return push(qsend.at[4 + s, r], qgot.at[4 + s, r], q_sem, 8 + 2 * s + u, at(0, 7, 0))

    def q_step(s):
        for u in range(2):
            r = slice(128 * u, 128 * u + 128)
            mine = dq[(z + 4 - s) % 8, r]
            if s:
                q_right(s - 1, u).wait_recv()
                mine = mine + qgot[s - 1, r]
            qsend[s, r] = mine
            q_right(s, u).start()
            if s < 3:
                mine = dq[(z + 5 + s) % 8, r]
                if s:
                    q_left(s - 1, u).wait_recv()
                    mine = mine + qgot[4 + s - 1, r]
                qsend[4 + s, r] = mine
                q_left(s, u).start()

    total = blocks(0, jnp.zeros((512, 256), f32))
    q_step(0)
    total = lax.fori_loop(1, 4, blocks, total)
    dsend[1] = total[256:512]
    to_sib[1].start()
    q_step(1)
    to_sib[1].wait_recv()
    mine = total[0:256] + dgot[1]
    across.wait_recv()
    d = mine + dgot[2]
    emb = items[0]
    d = inv_norm * (d - emb * jnp.sum(emb * d, axis=1, keepdims=True))

    for h in range(2):
        draw[h] = d[:, h * 128 : (h + 1) * 128]
        d_all[h, p] = d[:, h * 128 : (h + 1) * 128]

    def d_cp(h, i):
        return push(draw.at[h], d_all.at[h, p], d_sem, h * 7 + i, pbdev(*order[i]))

    for h in range(2):
        for i in range(7):
            d_cp(h, i).start()

    def add_rows(h, b, first):
        dcat = jnp.concatenate(split(d_all[h, b]), axis=1)
        for a in range(2):
            r = dot(ct[b, a * 1024 : (a + 1) * 1024, :], dcat)
            r = (r[:, 0:128] + r[:, 128:256]).reshape(8, 2, 64, 128)
            acc[h, a] = r if first else acc[h, a] + r

    def c_cp(h):
        return push(acc.at[h, :, :, 1 - core], cgot.at[h], c_sem, h, at(0, 0, 1))

    def e_cp(h, k):
        a, d = others[k]
        src = esum.at[h, (yh + a) % 2, (z + d) % 8]
        return push(src, egot.at[h, k], e_sem, h * 15 + k, at(a, d, 0))

    def send_rows(h):
        c_cp(h).wait_recv()
        esum[h] = acc[h, :, :, core] + cgot[h]
        for k in range(15):
            e_cp(h, k).start()

    add_rows(0, p, True)
    add_rows(1, p, True)
    for i in range(7):
        if i == 0:
            q_step(2)
        if i == 2:
            q_step(3)
        d_cp(0, i).wait_recv()
        add_rows(0, pb_from[i], False)
    c_cp(0).start()
    send_rows(0)
    for i in range(7):
        d_cp(1, i).wait_recv()
        add_rows(1, pb_from[i], False)
    c_cp(1).start()
    send_rows(1)
    for u in range(2):
        q_right(3, u).wait_recv()
        q_left(2, u).wait_recv()
    d = jnp.transpose(dq[z] + (qgot[3] + qgot[6]))
    qraw = qraw_s[...]
    inv_norm = lax.rsqrt(jnp.sum(qraw * qraw, axis=1, keepdims=True) + epsilon)
    emb = qraw * inv_norm
    d = inv_norm * (d - emb * jnp.sum(emb * d, axis=1, keepdims=True))
    d = dot3(d, qo_ref[...], NT) * gelu_slope(qpre_s[...])
    qg_ref[...] = dot3(d, qi_ref[...], NT)
    for h in range(2):
        for k in range(15):
            e_cp(h, k).wait_recv()
        v = esum[h, yh, z]
        for k in range(15):
            v = v + egot[h, k]
        vcat[:, h * 128 : (h + 1) * 128] = v
    d = dot(lhs(vcat[...]), outr[...], NT) * slope[...]
    tg_ref[...] = dot(lhs(d), innr[...], NT)

    for c in refs_cp + pos_cp + item_cp + to_sib + [across]:
        c.wait_send()
    for s in range(4):
        right(s).wait_send()
        q_right(s, 0).wait_send()
        q_right(s, 1).wait_send()
    for s in range(3):
        left(s).wait_send()
        q_left(s, 0).wait_send()
        q_left(s, 1).wait_send()
    for s in range(7):
        part_cp(s).wait_send()
    for h in range(2):
        c_cp(h).wait_send()
        for i in range(7):
            d_cp(h, i).wait_send()
        for k in range(15):
            e_cp(h, k).wait_send()


def keep_kernel(a_ref, b_ref, c_ref, a_out, b_out, c_out):
    a_out[...] = a_ref[...]
    b_out[...] = b_ref[...]
    c_out[...] = c_ref[...]


def per_device(
    query_feats,
    item_table,
    serve_ids,
    block_counts,
    item_refs,
    positive,
    query_inner,
    query_outer,
    item_inner,
    item_outer,
):
    vm = pl.BlockSpec(memory_space=pltpu.VMEM)
    sm = pl.BlockSpec(memory_space=pltpu.SMEM)
    hbm = pl.BlockSpec(memory_space=pl.ANY)
    loss, query_grad, table_grad = pl.pallas_call(
        step_kernel,
        name="step",
        out_shape=[
            jax.ShapeDtypeStruct((256,), f32),
            jax.ShapeDtypeStruct((256, 256), f32),
            jax.ShapeDtypeStruct((64, 256), f32),
        ],
        in_specs=[vm, sm, vm, vm] + [hbm] * 6,
        out_specs=[vm] * 3,
        scratch_shapes=[
            VM((2048, 256), f32),
            VM((256, 512), f32),
            VM((512, 256), f32),
            VM((256, 256), f32),
            VM((256, 512), f32),
            VM((512, 256), f32),
            VM((8, 256), jnp.int32),
            VM((8, 8, 256), jnp.int32),
            VM((8, 256), jnp.int32),
            VM((8, 8, 256), jnp.int32),
            VM((512, 2048), bf16),
            VM((512, 768), bf16),
            VM((256, 1536), bf16),
            VM((8, 256, 256), f32),
            VM((256, 512), f32),
            VM((256, 256), f32),
            VM((8, 2048, 256), bf16),
            VM((7, 256, 256), f32),
            VM((8, 256, 256), f32),
            VM((4, 256, 256), f32),
            VM((8, 256, 768), bf16),
            VM((8, 768, 256), bf16),
            VM((2, 256, 1536), bf16),
            VM((2, 8, 512, 256), f32),
            VM((16, 256), f32),
            VM((8, 16, 256), f32),
            VM((3, 256, 256), f32),
            VM((3, 256, 256), f32),
            VM((2, 256, 128), f32),
            VM((2, 8, 256, 128), f32),
            VM((8, 256, 256), f32),
            VM((2, 2, 8, 2, 64, 128), f32),
            VM((2, 2, 8, 64, 128), f32),
            VM((2, 2, 8, 64, 128), f32),
            VM((2, 15, 64, 128), f32),
            VM((64, 256), f32),
            VM((512, 768), bf16),
            VM((256, 1536), bf16),
            VM((64, 512), f32),
            VM((7, 256, 256), f32),
            VM((7, 256, 256), f32),
            DMA((6,)),
            DMA((2, 7)),
            DMA((2, 7)),
            DMA((2, 7)),
            DMA((2, 4)),
            DMA((2, 7)),
            DMA((2, 3)),
            DMA((2, 7)),
            DMA((2, 3)),
            DMA((2, 14)),
            DMA((2, 2)),
            DMA((2, 30)),
            DMA((2, 14)),
        ],
        compiler_params=pltpu.CompilerParams(
            collective_id=1, has_side_effects=True, vmem_limit_bytes=60 << 20
        ),
    )(
        item_refs.T,
        block_counts[0, 0],
        serve_ids[0, 0],
        positive.reshape(1, 256),
        item_table,
        item_inner,
        item_outer,
        query_feats,
        query_inner,
        query_outer,
    )
    return pl.pallas_call(
        keep_kernel,
        name="keep",
        out_shape=[
            jax.ShapeDtypeStruct((256,), f32),
            jax.ShapeDtypeStruct((256, 256), f32),
            jax.ShapeDtypeStruct((64, 256), f32),
        ],
        in_specs=[vm] * 3,
        out_specs=[vm] * 3,
    )(loss, query_grad, table_grad)


def solution(mesh):
    placed = (
        P(("pb", "ia"), None),
        P("pb", None),
        P("pb", "ia", None, None),
        P("pb", "ia", None),
        P(("pb", "ia"), None),
        P(("pb", "ia")),
        P(),
        P(),
        P(),
        P(),
    )
    return jax.shard_map(
        per_device,
        mesh=mesh,
        in_specs=placed,
        out_specs=(P(("pb", "ia")), P(("pb", "ia"), None), P(("pb", "ia"), None)),
        check_vma=False,
    )
```

```python
import jax
import jax.numpy as jnp
from jax import lax
from jax.experimental import pallas as pl
from jax.experimental.pallas import tpu as pltpu
from jax.sharding import PartitionSpec as P

BLOCK = 128
CAP = 512
MESH = pl.DeviceIdType.MESH
VM = pltpu.VMEM
DMA = pltpu.SemaphoreType.DMA
f32 = jnp.float32
bf16 = jnp.bfloat16

inverse_temp = 20.0
epsilon = 1e-06

NN = (((1,), (0,)), ((), ()))
NT = (((1,), (1,)), ((), ()))


def split(v):
    hi = v.astype(bf16)
    return hi, (v - hi.astype(f32)).astype(bf16)


def dot(a, b, dims=NN):
    return lax.dot_general(a, b, dims, preferred_element_type=f32)


def lhs(v):
    h, l = split(v)
    return jnp.concatenate([h, h, l], axis=1)


def rhs(v, axis):
    h, l = split(v)
    return jnp.concatenate([h, l, h], axis=axis)


def dot3(a, b, dims=NN):
    return dot(lhs(a), rhs(b, dims[0][1][0]), dims)


def normal_cdf(v):
    return 0.5 * (1.0 + lax.erf(v * 0.7071067811865476))


def gelu(v):
    return v * normal_cdf(v)


def gelu_slope(v):
    return normal_cdf(v) + v * (0.3989422804014327 * jnp.exp(-0.5 * v * v))


def place():
    p, j = lax.axis_index("pb"), lax.axis_index("ia")
    return p, j, p % 4, p // 4, j // 16, (j // 2) % 8, j % 2


def greet(peers):
    barrier = pltpu.get_barrier_semaphore()
    for peer in peers:
        pl.semaphore_signal(barrier, inc=1, device_id=peer, device_id_type=MESH)
    pl.semaphore_wait(barrier, len(peers))


def push(src, dst, sems, k, peer):
    return pltpu.make_async_remote_copy(
        src_ref=src,
        dst_ref=dst,
        send_sem=sems.at[0, k],
        recv_sem=sems.at[1, k],
        device_id=peer,
        device_id_type=MESH,
    )


def step_kernel(
    refs_ref,
    counts_ref,
    lists_ref,
    pos_ref,
    table_hbm,
    inner_hbm,
    outer_hbm,
    qf_hbm,
    qi_hbm,
    qo_hbm,
    loss_ref,
    qg_ref,
    tg_ref,
    table_ref,
    inner_ref,
    outer_ref,
    qf_ref,
    qi_ref,
    qo_ref,
    live,
    refs_all,
    posb,
    pos_all,
    zcat,
    inncat,
    outcat,
    qall,
    qpre_s,
    qraw_s,
    ct,
    part,
    got,
    items,
    qn,
    qr,
    tcat,
    ex,
    stats,
    stats_all,
    dsend,
    dgot,
    draw,
    d_all,
    dq,
    acc,
    cgot,
    esum,
    egot,
    vcat,
    outr,
    innr,
    slope,
    qsend,
    qgot,
    load_sem,
    refs_sem,
    pos_sem,
    ring_sem,
    zt_sem,
    part_sem,
    item_sem,
    stat_sem,
    near_sem,
    d_sem,
    c_sem,
    e_sem,
    q_sem,
):
    p, j, x, yl, yh, z, core = place()
    loads = [
        pltpu.make_async_copy(src, dst, load_sem.at[i])
        for i, (src, dst) in enumerate(
            [
                (qf_hbm, qf_ref),
                (qi_hbm, qi_ref),
                (qo_hbm, qo_ref),
                (inner_hbm, inner_ref),
                (outer_hbm, outer_ref),
                (table_hbm, table_ref),
            ]
        )
    ]
    for c in loads:
        c.start()

    def at(dyh, dz, dc):
        return (p, (((yh + dyh) % 2) * 8 + (z + dz) % 8) * 2 + (core + dc) % 2)

    def pbdev(dy, dx):
        return (((yl + dy) % 2) * 4 + (x + dx) % 4, j)

    order = [(1, 0), (0, 1), (0, 3), (0, 2), (1, 1), (1, 3), (1, 2)]
    pb_from = [((yl + dy) % 2) * 4 + (x + 4 - dx) % 4 for dy, dx in order]
    others = [(a, d) for d in (4, 3, 5, 2, 6, 1, 7, 0) for a in (0, 1) if a or d]
    greet(
        [pbdev(*d) for d in order]
        + [at(a, d, 0) for a, d in others]
        + [at(0, 0, 1)]
    )

    refs = refs_ref[...]
    owner = refs // CAP
    limit = jnp.zeros((8, 256), jnp.int32)
    for o in range(8):
        limit = jnp.where(owner == o, BLOCK * counts_ref[o], limit)
    live[...] = jnp.where(refs - owner * CAP < limit, refs, -1)
    refs_all[p] = live[...]
    posb[...] = jnp.broadcast_to(pos_ref[...], (8, 256))
    pos_all[z] = posb[...]
    refs_cp = [push(live, refs_all.at[p], refs_sem, i, pbdev(*d)) for i, d in enumerate(order)]
    pos_cp = [push(posb, pos_all.at[z], pos_sem, i, at(0, i + 1, 0)) for i in range(7)]
    for c in refs_cp + pos_cp:
        c.start()

    for c in loads[:3]:
        c.wait()
    qpre = dot3(qf_ref[...], qi_ref[...])
    qpre_s[...] = qpre
    qraw = dot3(gelu(qpre), qo_ref[...])
    qraw_s[...] = qraw
    qall[z] = qraw * lax.rsqrt(jnp.sum(qraw * qraw, axis=1, keepdims=True) + epsilon)

    def right(s):
        b = (z + 8 - s) % 8
        return push(qall.at[b], qall.at[b], ring_sem, s, at(0, 1, 0))

    def left(s):
        b = (z + s) % 8
        return push(qall.at[b], qall.at[b], ring_sem, 4 + s, at(0, 7, 0))

    def ring(s):
        if s:
            right(s - 1).wait_recv()
            if s < 4:
                left(s - 1).wait_recv()
        right(s).start()
        if s < 3:
            left(s).start()

    ring(0)

    for c in loads[3:]:
        c.wait()
    inncat[...] = lhs(jnp.transpose(inner_ref[...]))
    outcat[...] = lhs(jnp.transpose(outer_ref[...]))

    def share(i):
        t = core * 4 + i
        return push(dq.at[t], dq.at[t], zt_sem, i, at(0, 0, 1))

    def keep(t):
        r = pl.ds(pl.multiple_of(t * 256, 256), 256)
        h, l = split(dq[t])
        zcat[0:256, r] = h
        zcat[256:512, r] = l

    def rows(i, carry):
        t = core * 4 + i
        r = pl.ds(pl.multiple_of(t * 256, 256), 256)
        hid = dot(inncat[...], rhs(table_ref[r, :], 1), NT)
        dq[t] = dot(outcat[...], rhs(gelu(hid), 0))
        share(i).start()
        keep(t)
        return carry

    lax.fori_loop(0, 4, rows, 0, unroll=2)
    ring(1)
    for i in range(4):
        share(i).wait_recv()
        keep((1 - core) * 4 + i)
    for i in range(4):
        share(i).wait_send()

    for c in refs_cp:
        c.wait_recv()

    def piece(s):
        k = s // 2
        dx = (1 - k // 2) * (2 + k) + (k // 2) * (3 - k)
        dy = 1 - s % 2
        return pbdev(dy, dx)

    def part_cp(s):
        return push(part.at[s], got.at[p], part_sem, s, piece(s))

    def pieces(s, carry):
        b = piece(s)[0]
        refs = refs_all[b]
        slot = lax.broadcasted_iota(jnp.int32, (CAP, 256), 0) + p * CAP
        uses = jnp.zeros((CAP, 256), f32)
        for k in range(8):
            uses = uses + jnp.where(slot == refs[k : k + 1, :], 1.0, 0.0)
        uses = uses.astype(bf16)
        listed = lists_ref[pl.ds(b, 1), :]
        for t in range(2):
            row = lax.broadcasted_iota(jnp.int32, (1024, CAP), 0) + t * 1024
            pick = jnp.where(row == listed, 1.0, 0.0).astype(bf16)
            ct[b, t * 1024 : (t + 1) * 1024, :] = dot(pick, uses).astype(bf16)
        total = dot(zcat[...], ct[b])
        total = total[0:256] + total[256:512]

        @pl.when(s < 7)
        def _():
            part[s] = total
            part_cp(s).start()

        @pl.when(s == 7)
        def _():
            got[p] = total

        return carry

    lax.fori_loop(0, 4, pieces, 0)
    ring(2)
    lax.fori_loop(4, 8, pieces, 0)
    ring(3)
    right(3).wait_recv()

    def queries(b, carry):
        q = qall[b]
        qn[b] = rhs(q, 1)
        qr[b] = rhs(q, 0)
        return carry

    lax.fori_loop(0, 8, queries, 0)
    raw = got[p]
    for s in range(7):
        part_cp(s).wait_recv()
        dx = (2, 3, 1, 0)[s // 2]
        raw = raw + got[((yl + 1 - s % 2) % 2) * 4 + (x + 4 - dx) % 4]
    raw = jnp.transpose(raw)
    inv_norm = lax.rsqrt(jnp.sum(raw * raw, axis=1, keepdims=True) + epsilon)
    items[0] = raw * inv_norm

    item_cp = [
        push(items.at[0], items.at[2], item_sem, 1, at(1, 0, 0)),
        push(items.at[0], items.at[1], item_sem, 0, at(0, 0, 1)),
        push(items.at[2], items.at[3], item_sem, 2, at(0, 0, 1)),
    ]
    item_cp[0].start()
    item_cp[1].start()
    stats[...] = jnp.zeros((16, 256), f32)

    def numbers(i):
        row = lax.broadcasted_iota(jnp.int32, (512, 256), 0)
        a = ((yh + i) % 2) * 16 + z * 2
        first, second = (a + core) * 256, (a + 1 - core) * 256 - 256
        return row + jnp.where(row < 256, first, second)

    def logits(i, first, last):
        if last - first == 512:
            here = lhs(items[2 * i : 2 * i + 2].reshape(512, 256))
        else:
            here = lhs(items[2 * i + first // 256])
        number = numbers(i)[first:last]

        def step(b, carry):
            lg = inverse_temp * dot(here, qn[b], NT)
            e = jnp.exp(lg)
            ex[i, b, first:last] = e
            r = pl.ds(b, 1)
            stats[r, :] = stats[r, :] + jnp.sum(e, axis=0, keepdims=True)
            hit = pos_all[b][0:1, :] == number
            r8 = pl.ds(b + 8, 1)
            stats[r8, :] = stats[r8, :] + jnp.sum(jnp.where(hit, lg, 0.0), axis=0, keepdims=True)
            return carry

        lax.fori_loop(0, 8, step, 0)

    for c in pos_cp:
        c.wait_recv()
    item_cp[1].wait_recv()
    logits(0, 0, 512)
    item_cp[0].wait_recv()
    item_cp[2].start()
    logits(1, 0, 256)
    item_cp[2].wait_recv()
    logits(1, 256, 512)

    upper, lower = pl.ds(0, 8), pl.ds(8, 8)
    stat_cp = [
        push(stats.at[r], stats_all.at[z, r], stat_sem, 7 * k + i, at(0, i + 1, 0))
        for k, r in enumerate((upper, lower))
        for i in (3, 2, 4, 1, 5, 0, 6)
    ]
    for c in stat_cp:
        c.start()
    stats_all[z] = stats[...]
    for i in range(2):
        h, l = split(jnp.transpose(items[2 * i : 2 * i + 2].reshape(512, 256)))
        tcat[i] = jnp.concatenate([h, l, h], axis=1)
    outr[...] = rhs(outer_ref[...], 1)
    innr[...] = rhs(inner_ref[...], 1)
    own = table_ref[pl.ds(pl.multiple_of(j * 64, 64), 64), :]
    slope[...] = gelu_slope(dot3(own, inner_ref[...]))
    for c in stat_cp[:7]:
        c.wait()
    sums = stats_all[0, 0:8]
    for b in range(1, 8):
        sums = sums + stats_all[b, 0:8]
    stats_all[z, 0:8] = sums
    stats[0:8, :] = inverse_temp / sums

    def coefficients(i, b):
        hit = pos_all[b][0:1, :] == numbers(i)
        return split(ex[i, b] * stats[pl.ds(b, 1), :] - jnp.where(hit, inverse_temp, 0.0))

    def item_part(c, b):
        return dot(jnp.concatenate([c[0], c[0], c[1]], axis=1), qr[b])

    def far_items(first):
        def step(b, total):
            hit = pos_all[b][0:1, :] == numbers(1)[first : first + 256]
            c = ex[1, b, first : first + 256] * stats[pl.ds(b, 1), :]
            return total + item_part(split(c - jnp.where(hit, inverse_temp, 0.0)), b)

        return lax.fori_loop(0, 8, step, jnp.zeros((256, 256), f32), unroll=2)

    to_sib = [push(dsend.at[i], dgot.at[i], near_sem, i, at(0, 0, 1)) for i in range(2)]
    across = push(dsend.at[2], dgot.at[2], near_sem, 2, at(1, 0, 0))
    dsend[0] = far_items(256)
    to_sib[0].start()
    total = far_items(0)
    to_sib[0].wait_recv()
    dsend[2] = total + dgot[0]
    across.start()

    def both_sides(b, total):
        c0, c1 = coefficients(0, b), coefficients(1, b)
        dq[b] = dot(tcat[0], jnp.concatenate([c0[0], c0[0], c0[1]], axis=0)) + dot(
            tcat[1], jnp.concatenate([c1[0], c1[0], c1[1]], axis=0)
        )
        return total + item_part(c0, b)

    def blocks(s, total):
        return both_sides((z + 5 + s) % 8, both_sides((z + 4 - s) % 8, total))

    def q_right(s, u):
        r = pl.ds(128 * u, 128)
        return push(qsend.at[s, r], qgot.at[s, r], q_sem, 2 * s + u, at(0, 1, 0))

    def q_left(s, u):
        r = pl.ds(128 * u, 128)
        return push(qsend.at[4 + s, r], qgot.at[4 + s, r], q_sem, 8 + 2 * s + u, at(0, 7, 0))

    def q_step(s):
        for u in range(2):
            r = slice(128 * u, 128 * u + 128)
            mine = dq[(z + 4 - s) % 8, r]
            if s:
                q_right(s - 1, u).wait_recv()
                mine = mine + qgot[s - 1, r]
            qsend[s, r] = mine
            q_right(s, u).start()
            if s < 3:
                mine = dq[(z + 5 + s) % 8, r]
                if s:
                    q_left(s - 1, u).wait_recv()
                    mine = mine + qgot[4 + s - 1, r]
                qsend[4 + s, r] = mine
                q_left(s, u).start()

    total = blocks(0, jnp.zeros((512, 256), f32))
    q_step(0)
    total = lax.fori_loop(1, 4, blocks, total)
    dsend[1] = total[256:512]
    to_sib[1].start()
    q_step(1)
    for c in stat_cp[7:]:
        c.wait()
    loss = jnp.log(stats_all[z, pl.ds(z, 1), :])
    for b in range(8):
        loss = loss - stats_all[b, pl.ds(z + 8, 1), :]
    loss_ref[...] = loss.reshape(256)
    to_sib[1].wait_recv()
    mine = total[0:256] + dgot[1]
    across.wait_recv()
    d = mine + dgot[2]
    emb = items[0]
    d = inv_norm * (d - emb * jnp.sum(emb * d, axis=1, keepdims=True))

    for h in range(2):
        draw[h] = d[:, h * 128 : (h + 1) * 128]
        d_all[h, p] = d[:, h * 128 : (h + 1) * 128]

    def d_cp(h, i):
        return push(draw.at[h], d_all.at[h, p], d_sem, h * 7 + i, pbdev(*order[i]))

    for h in range(2):
        for i in range(7):
            d_cp(h, i).start()

    def add_rows(h, b, first):
        dcat = jnp.concatenate(split(d_all[h, b]), axis=1)
        for a in range(2):
            r = dot(ct[b, a * 1024 : (a + 1) * 1024, :], dcat)
            r = (r[:, 0:128] + r[:, 128:256]).reshape(8, 2, 64, 128)
            acc[h, a] = r if first else acc[h, a] + r

    def c_cp(h):
        return push(acc.at[h, :, :, 1 - core], cgot.at[h], c_sem, h, at(0, 0, 1))

    def e_cp(h, k):
        a, d = others[k]
        src = esum.at[h, (yh + a) % 2, (z + d) % 8]
        return push(src, egot.at[h, k], e_sem, h * 15 + k, at(a, d, 0))

    def send_rows(h):
        c_cp(h).wait_recv()
        esum[h] = acc[h, :, :, core] + cgot[h]
        for k in range(15):
            e_cp(h, k).start()

    add_rows(0, p, True)
    add_rows(1, p, True)
    for i in range(7):
        if i == 0:
            q_step(2)
        if i == 2:
            q_step(3)
        d_cp(0, i).wait_recv()
        add_rows(0, pb_from[i], False)
    c_cp(0).start()
    send_rows(0)
    for i in range(7):
        d_cp(1, i).wait_recv()
        add_rows(1, pb_from[i], False)
    c_cp(1).start()
    send_rows(1)
    for u in range(2):
        q_right(3, u).wait_recv()
        q_left(2, u).wait_recv()
    d = jnp.transpose(dq[z] + (qgot[3] + qgot[6]))
    qraw = qraw_s[...]
    inv_norm = lax.rsqrt(jnp.sum(qraw * qraw, axis=1, keepdims=True) + epsilon)
    emb = qraw * inv_norm
    d = inv_norm * (d - emb * jnp.sum(emb * d, axis=1, keepdims=True))
    d = dot3(d, qo_ref[...], NT) * gelu_slope(qpre_s[...])
    qg_ref[...] = dot3(d, qi_ref[...], NT)
    for h in range(2):
        for k in range(15):
            e_cp(h, k).wait_recv()
        v = esum[h, yh, z]
        for k in range(15):
            v = v + egot[h, k]
        vcat[:, h * 128 : (h + 1) * 128] = v
    d = dot(lhs(vcat[...]), outr[...], NT) * slope[...]
    tg_ref[...] = dot(lhs(d), innr[...], NT)

    for c in refs_cp + pos_cp + item_cp + to_sib + [across]:
        c.wait_send()
    for s in range(4):
        right(s).wait_send()
        q_right(s, 0).wait_send()
        q_right(s, 1).wait_send()
    for s in range(3):
        left(s).wait_send()
        q_left(s, 0).wait_send()
        q_left(s, 1).wait_send()
    for s in range(7):
        part_cp(s).wait_send()
    for h in range(2):
        c_cp(h).wait_send()
        for i in range(7):
            d_cp(h, i).wait_send()
        for k in range(15):
            e_cp(h, k).wait_send()


def keep_kernel(a_ref, b_ref, c_ref, a_out, b_out, c_out):
    a_out[...] = a_ref[...]
    b_out[...] = b_ref[...]
    c_out[...] = c_ref[...]


def per_device(
    query_feats,
    item_table,
    serve_ids,
    block_counts,
    item_refs,
    positive,
    query_inner,
    query_outer,
    item_inner,
    item_outer,
):
    vm = pl.BlockSpec(memory_space=pltpu.VMEM)
    sm = pl.BlockSpec(memory_space=pltpu.SMEM)
    hbm = pl.BlockSpec(memory_space=pl.ANY)
    loss, query_grad, table_grad = pl.pallas_call(
        step_kernel,
        name="step",
        out_shape=[
            jax.ShapeDtypeStruct((256,), f32),
            jax.ShapeDtypeStruct((256, 256), f32),
            jax.ShapeDtypeStruct((64, 256), f32),
        ],
        in_specs=[vm, sm, vm, vm] + [hbm] * 6,
        out_specs=[vm] * 3,
        scratch_shapes=[
            VM((2048, 256), f32),
            VM((256, 512), f32),
            VM((512, 256), f32),
            VM((256, 256), f32),
            VM((256, 512), f32),
            VM((512, 256), f32),
            VM((8, 256), jnp.int32),
            VM((8, 8, 256), jnp.int32),
            VM((8, 256), jnp.int32),
            VM((8, 8, 256), jnp.int32),
            VM((512, 2048), bf16),
            VM((512, 768), bf16),
            VM((256, 1536), bf16),
            VM((8, 256, 256), f32),
            VM((256, 512), f32),
            VM((256, 256), f32),
            VM((8, 2048, 256), bf16),
            VM((7, 256, 256), f32),
            VM((8, 256, 256), f32),
            VM((4, 256, 256), f32),
            VM((8, 256, 768), bf16),
            VM((8, 768, 256), bf16),
            VM((2, 256, 1536), bf16),
            VM((2, 8, 512, 256), f32),
            VM((16, 256), f32),
            VM((8, 16, 256), f32),
            VM((3, 256, 256), f32),
            VM((3, 256, 256), f32),
            VM((2, 256, 128), f32),
            VM((2, 8, 256, 128), f32),
            VM((8, 256, 256), f32),
            VM((2, 2, 8, 2, 64, 128), f32),
            VM((2, 2, 8, 64, 128), f32),
            VM((2, 2, 8, 64, 128), f32),
            VM((2, 15, 64, 128), f32),
            VM((64, 256), f32),
            VM((512, 768), bf16),
            VM((256, 1536), bf16),
            VM((64, 512), f32),
            VM((7, 256, 256), f32),
            VM((7, 256, 256), f32),
            DMA((6,)),
            DMA((2, 7)),
            DMA((2, 7)),
            DMA((2, 7)),
            DMA((2, 4)),
            DMA((2, 7)),
            DMA((2, 3)),
            DMA((2, 14)),
            DMA((2, 3)),
            DMA((2, 14)),
            DMA((2, 2)),
            DMA((2, 30)),
            DMA((2, 14)),
        ],
        compiler_params=pltpu.CompilerParams(
            collective_id=1, has_side_effects=True, vmem_limit_bytes=60 << 20
        ),
    )(
        item_refs.T,
        block_counts[0, 0],
        serve_ids[0, 0],
        positive.reshape(1, 256),
        item_table,
        item_inner,
        item_outer,
        query_feats,
        query_inner,
        query_outer,
    )
    return pl.pallas_call(
        keep_kernel,
        name="keep",
        out_shape=[
            jax.ShapeDtypeStruct((256,), f32),
            jax.ShapeDtypeStruct((256, 256), f32),
            jax.ShapeDtypeStruct((64, 256), f32),
        ],
        in_specs=[vm] * 3,
        out_specs=[vm] * 3,
    )(loss, query_grad, table_grad)


def solution(mesh):
    placed = (
        P(("pb", "ia"), None),
        P("pb", None),
        P("pb", "ia", None, None),
        P("pb", "ia", None),
        P(("pb", "ia"), None),
        P(("pb", "ia")),
        P(),
        P(),
        P(),
        P(),
    )
    return jax.shard_map(
        per_device,
        mesh=mesh,
        in_specs=placed,
        out_specs=(P(("pb", "ia")), P(("pb", "ia"), None), P(("pb", "ia"), None)),
        check_vma=False,
    )
```
